256 devices in a mesh: ctx: 16 (over y_lo, x, core), head: 16 (over z, y_hi).
Axes of the slice: x: 4, y: 4 (y_hi: 2, y_lo: 2; y = y_hi * 2 + y_lo), z: 8, core: 2. Of those that a mesh axis runs over, the one named last changes fastest.
Arguments:
- queries: bfloat16 [6144, 8192], P('ctx', 'head'), may hold values from -6 to 6
- out_grad: bfloat16 [6144, 8192], P('ctx', 'head'), may hold values from -6 to 6
- outputs: bfloat16 [6144, 8192], P('ctx', 'head'), may hold values from -6 to 6
- lse: float32 [64, 6144], P('head', 'ctx'), may hold values from 4.5 to 6.5
- kv_pair: bfloat16 [16, 6144, 128], P('head', 'ctx'), may hold values from -6 to 6
- span_order: int32 [32], replicated, may hold values from 0 to 31, as said below
- doc_start: int32 [6144], P('ctx'), may hold values from 0 to 6143, as said below
Outputs:
- query_grad: bfloat16 [6144, 8192], P('ctx', 'head')
- kv_grad: bfloat16 [16, 6144, 128], P('head', 'ctx')
The draws below stay inside these ranges and needn't reach their ends.
Inputs may be any that keep to these rules, and one draw needn't show every extreme that they name: `span_order`: each of 0 to 31 appears once. Documents are runs of consecutive positions, at most 4 of them, the first starting at position 0 and the last position 6143 a document of its own; doc_start of a row is at most its position.
All inputs are finite; a program needn't handle non-finite values.
Results may differ from the reference program's by a relative error of at most 0.0049.
Values may be sent and summed in bfloat16 or wider, within the bound.
No kernel may reach another device: no remote copies, remote signals or barrier semaphores. Data moves between devices by JAX's collectives and lax.ppermute only.
A program may use at most 64 MiB of HBM per device.

```python
import math
import jax
import jax.numpy as jnp
from jax import lax

HD = 128
GROUP = 8
CH = 192
KVH = 8
QH = 64
TOKENS = 6144


def layout_draw(key):
    order_key, cut_key = jax.random.split(key)
    span_count = TOKENS // CH
    span_order = jax.random.permutation(order_key, span_count).astype(jnp.int32)
    cuts = jax.random.randint(cut_key, (2,), 1, TOKENS - 1).astype(jnp.int32)
    final_cut = jnp.full((1,), TOKENS - 1, jnp.int32)
    starts = jnp.concatenate([jnp.zeros((1,), jnp.int32), cuts, final_cut])
    row_index = jnp.arange(TOKENS, dtype=jnp.int32)
    positions = span_order[row_index // CH] * CH + row_index % CH
    covered = starts[None, :] <= positions[:, None]
    doc_start = jnp.max(jnp.where(covered, starts[None, :], 0), axis=1).astype(jnp.int32)
    return (span_order, doc_start)


def draw_span_order(key, part):
    span_order, doc_start = layout_draw(key)
    return span_order


def draw_doc_start(key, part):
    span_order, doc_start = layout_draw(key)
    return doc_start


def levels(stream_key, extent, cuts, smallest, largest):
    def one(dim, parts):
        heights = jax.random.uniform(jax.random.fold_in(jax.random.fold_in(stream_key, 6), dim), (parts,), jnp.float32, smallest / len(cuts), largest / len(cuts))
        return jnp.repeat(jnp.exp(heights), extent[dim] // parts).reshape((-1,) + (1,) * (len(extent) - dim - 1))

    gain = one(*cuts[0])
    for cut in cuts[1:]:
        gain = gain * one(*cut)
    return gain


def centred(key, extent, scale, reach, cuts=(), kind=jnp.bfloat16):
    level = levels(key, extent, cuts, -0.22, 0.18) if cuts else 1.0
    values = jax.random.normal(key, extent, jnp.float32) * scale * level
    return jnp.minimum(jnp.maximum(values, -reach), reach).astype(kind)


def setup_inputs(seed: int = 0) -> dict:
    seeds = jax.random.split(jax.random.key(seed), 8)
    return {
        "queries": centred(seeds[0], (TOKENS, QH * HD), 1.0, 6.0, ((0, 16), (1, 16))),
        "out_grad": centred(seeds[1], (TOKENS, QH * HD), 1.0, 6.0, ((0, 16), (1, 16))),
        "outputs": centred(seeds[2], (TOKENS, QH * HD), 1.0, 6.0, ((0, 16), (1, 16))),
        "lse": jnp.clip(4.5 + 2.0 * jax.random.uniform(seeds[3], (QH, TOKENS), jnp.float32) ** levels(seeds[3], (QH, TOKENS), ((0, 16), (1, 16)), -0.2, 0.2), 4.5, 6.5),
        "kv_pair": centred(seeds[4], (2 * KVH, TOKENS, HD), 1.0, 6.0, ((0, 16), (1, 16))),
        "span_order": draw_span_order(jax.random.fold_in(seeds[7], 71), 0),
        "doc_start": draw_doc_start(jax.random.fold_in(seeds[7], 71), 0),
    }


def grads_block(q_block, g_block, lse_block, delta_block, q_positions, q_starts, key_block, value_block, k_positions, scale_factor):
    row_count, head_count, head_dim = q_block.shape
    key_count = key_block.shape[0]
    q_flat = q_block.astype(jnp.float32).reshape(row_count * head_count, head_dim)
    g_flat = g_block.astype(jnp.float32).reshape(row_count * head_count, head_dim)
    key_wide = key_block.astype(jnp.float32)
    value_wide = value_block.astype(jnp.float32)
    scores = jnp.dot(q_flat, key_wide.T, preferred_element_type=jnp.float32).reshape(row_count, head_count, key_count) * scale_factor
    allowed = (k_positions[None, :] <= q_positions[:, None]) & (k_positions[None, :].astype(jnp.float32) >= q_starts[:, None])
    probs = jnp.where(allowed[:, None, :], jnp.exp(scores - lse_block.T[:, :, None]), jnp.float32(0.0))
    probs_low = probs.astype(jnp.bfloat16).reshape(row_count * head_count, key_count)
    value_grad = jnp.dot(probs_low.astype(jnp.float32).T, g_flat, preferred_element_type=jnp.float32)
    prob_grad = jnp.dot(g_flat, value_wide.T, preferred_element_type=jnp.float32).reshape(row_count, head_count, key_count)
    score_grad = (probs * (prob_grad - delta_block.T[:, :, None])).astype(jnp.bfloat16).reshape(row_count * head_count, key_count)
    score_wide = score_grad.astype(jnp.float32)
    query_grad = (jnp.dot(score_wide, key_wide, preferred_element_type=jnp.float32) * scale_factor).reshape(row_count, head_count, head_dim)
    key_grad = jnp.dot(score_wide.T, q_flat, preferred_element_type=jnp.float32) * scale_factor
    return (query_grad, key_grad, value_grad)

def reference(queries, out_grad, outputs, lse, kv_pair, span_order, doc_start):
    token_count = queries.shape[0]
    head_count = lse.shape[0]
    head_dim = kv_pair.shape[2]
    span_rows = token_count // span_order.shape[0]
    row_index = jnp.arange(token_count, dtype=jnp.int32)
    positions = span_order[row_index // span_rows] * span_rows + row_index % span_rows
    starts = doc_start.astype(jnp.float32)
    query_heads = queries.reshape(token_count, head_count, head_dim)
    grad_heads = out_grad.reshape(token_count, head_count, head_dim)
    output_heads = outputs.reshape(token_count, head_count, head_dim)
    delta_rows = lax.optimization_barrier(jnp.sum(grad_heads.astype(jnp.float32) * output_heads.astype(jnp.float32), axis=2)).T
    scale_factor = 1.0 / math.sqrt(head_dim)

    def one_head(head):
        group_index = head // GROUP
        key_block = lax.dynamic_index_in_dim(kv_pair, 2 * group_index, 0, keepdims=False)
        value_block = lax.dynamic_index_in_dim(kv_pair, 2 * group_index + 1, 0, keepdims=False)
        q_block = lax.dynamic_slice_in_dim(query_heads, head, 1, 1)
        g_block = lax.dynamic_slice_in_dim(grad_heads, head, 1, 1)
        lse_block = lax.dynamic_slice_in_dim(lse, head, 1, 0)
        delta_block = lax.dynamic_slice_in_dim(delta_rows, head, 1, 0)
        q_grad, k_grad, v_grad = grads_block(q_block, g_block, lse_block, delta_block, positions, starts, key_block, value_block, positions, scale_factor)
        return (q_grad[:, 0, :], k_grad, v_grad)
    q_grads, k_grads, v_grads = lax.map(one_head, jnp.arange(head_count, dtype=jnp.int32))
    query_grad = jnp.transpose(q_grads, (1, 0, 2)).reshape(token_count, head_count * head_dim).astype(jnp.bfloat16)
    groups = head_count // GROUP
    key_sum = k_grads.reshape(groups, GROUP, token_count, head_dim).sum(axis=1)
    value_sum = v_grads.reshape(groups, GROUP, token_count, head_dim).sum(axis=1)
    kv_grad = jnp.stack([key_sum, value_sum], axis=1).reshape(2 * groups, token_count, head_dim).astype(jnp.bfloat16)
    return (query_grad, kv_grad)
```

```python
import functools
import math

import jax
import jax.numpy as jnp
from jax import lax
from jax.experimental import pallas as pl
from jax.experimental.pallas import tpu as pltpu
from jax.sharding import PartitionSpec as P

HEAD_DIM = 128
SPAN = 192
HEADS = 4
FLAT = HEADS * SPAN
LOG2E = math.log2(math.e)
SCALE = 1.0 / math.sqrt(HEAD_DIM)
AXES = ("ctx", "head")
NT = (((1,), (1,)), ((), ()))


def device_index(x, y, core, z):
    ctx = (y % 2) * 8 + x * 2 + core
    head = z * 2 + y // 2
    return ctx * 16 + head


def route(step_a, step_b):
    pairs = []
    for z in range(8):
        for y in range(4):
            for x in range(4):
                for core in range(2):
                    dx, dy = (step_a, step_b) if core == 0 else (step_b, step_a)
                    pairs.append(
                        (
                            device_index(x, y, core, z),
                            device_index((x + dx) % 4, (y + dy) % 4, core, z),
                        )
                    )
    return pairs


def move(block, step_a, step_b):
    return lax.ppermute(block, AXES, route(step_a, step_b))


def other_core(block):
    return lax.ppermute(block, "ctx", [(i, i ^ 1) for i in range(16)])


def grads_kernel(sched, *refs):
    q_refs, g_refs, stat_refs = refs[0:2], refs[2:4], refs[4:6]
    kv_refs = refs[6:22]
    dq_refs = refs[22:24]
    d0_ref, d1a_ref, d1b_ref, d2a_ref, d2b_ref, d3a_ref, d3b_ref = refs[24:31]
    q_flat, g_flat, kv_all, key_t, dq_t, dkv = refs[31:]

    for side in range(2):
        for half in range(2):
            rows = pl.ds(half * SPAN, SPAN)
            for h in range(HEADS):
                cols = pl.ds(h * HEAD_DIM, HEAD_DIM)
                out = pl.ds(h * SPAN, SPAN)
                q_flat[2 * side + half, out, :] = q_refs[side][rows, cols]
                g_flat[2 * side + half, out, :] = g_refs[side][rows, cols]
    for n in range(16):
        slot = sched[32 + n]
        kv_all[slot] = kv_refs[n][...]
    dq_t[...] = jnp.zeros_like(dq_t)
    dkv[...] = jnp.zeros_like(dkv)

    @pl.loop(0, 16)
    def _(ks):
        idx = ks // 2
        rows = pl.ds(pl.multiple_of((ks % 2) * SPAN, SPAN), SPAN)
        sk = sched[16 + ks]
        key_t[...] = kv_all[idx, rows, :].T

        def pair(qs, sq, masked):
            key = kv_all[idx, rows, :]
            value = kv_all[8 + idx, rows, :]
            q = q_flat[qs]
            g = g_flat[qs]
            side, half = qs // 2, qs % 2
            stat = stats_at(stat_refs, side, half)
            lse, delta = stat[0:1, :], stat[1:2, :]
            s = lax.dot_general(key, q, NT, preferred_element_type=jnp.float32)
            p = jnp.exp2(s * (SCALE * LOG2E) - lse)
            if masked:
                k_pos = lax.broadcasted_iota(jnp.int32, (SPAN, FLAT), 0) + sk * SPAN
                q_pos = stat[3:4, :].astype(jnp.int32) + sq * SPAN
                start = stat[2:3, :].astype(jnp.int32)
                p = jnp.where((k_pos <= q_pos) & (k_pos >= start), p, 0.0)
            p_low = p.astype(jnp.bfloat16)
            dkv[8 + idx, rows, :] += jnp.dot(p_low, g, preferred_element_type=jnp.float32)
            dp = lax.dot_general(value, g, NT, preferred_element_type=jnp.float32)
            ds = (p * (dp - delta)).astype(jnp.bfloat16)
            dkv[idx, rows, :] += jnp.dot(ds, q, preferred_element_type=jnp.float32)
            dq_t[qs] += jnp.dot(key_t[...], ds, preferred_element_type=jnp.float32)

        for qs in range(4):
            sq, first, last = sched[qs], sched[4 + qs], sched[8 + qs]
            active = (sk <= sq) & (sk * SPAN + (SPAN - 1) >= first)
            full = (sk < sq) & (sk * SPAN >= last)

            @pl.when(full)
            def _(qs=qs, sq=sq):
                pair(qs, sq, False)

            @pl.when(active & jnp.logical_not(full))
            def _(qs=qs, sq=sq):
                pair(qs, sq, True)

    for side in range(2):
        for half in range(2):
            flat = dq_t[2 * side + half].T * SCALE
            for h in range(HEADS):
                dq_refs[side][pl.ds(half * SPAN, SPAN), pl.ds(h * HEAD_DIM, HEAD_DIM)] = flat[
                    h * SPAN : (h + 1) * SPAN, :
                ]

    def partial(a, b):
        slot = sched[32 + 4 * a + b]
        factor = jnp.where(slot < 8, jnp.float32(SCALE), jnp.float32(1.0))
        return (dkv[slot] * factor).astype(jnp.bfloat16)

    for a in range(4):
        d0_ref[a] = partial(a, 0)
    for a in range(2):
        d1a_ref[a], d1b_ref[a] = partial(a, 1), partial(a + 2, 1)
        d2a_ref[a], d2b_ref[a] = partial(a, 2), partial(a + 2, 2)
        d3a_ref[a], d3b_ref[a] = partial(a, 3), partial(a + 2, 3)


def stats_at(stat_refs, side, half):
    return stat_refs[side][half]


def local_grads(sched, q, g, stats, kv):
    rows, width = q[0].shape
    vmem = pl.BlockSpec(memory_space=pltpu.VMEM)
    two = jax.ShapeDtypeStruct((2, rows, HEAD_DIM), jnp.bfloat16)
    four = jax.ShapeDtypeStruct((4, rows, HEAD_DIM), jnp.bfloat16)
    dq = jax.ShapeDtypeStruct((rows, width), jnp.float32)
    return pl.pallas_call(
        grads_kernel,
        out_shape=(dq, dq, four, two, two, two, two, two, two),
        in_specs=[pl.BlockSpec(memory_space=pltpu.SMEM)] + [vmem] * 22,
        out_specs=(vmem,) * 9,
        scratch_shapes=[
            pltpu.VMEM((4, FLAT, HEAD_DIM), jnp.bfloat16),
            pltpu.VMEM((4, FLAT, HEAD_DIM), jnp.bfloat16),
            pltpu.VMEM((16, rows, HEAD_DIM), jnp.bfloat16),
            pltpu.VMEM((HEAD_DIM, SPAN), jnp.bfloat16),
            pltpu.VMEM((4, HEAD_DIM, FLAT), jnp.float32),
            pltpu.VMEM((16, rows, HEAD_DIM), jnp.float32),
        ],
        compiler_params=pltpu.CompilerParams(vmem_limit_bytes=48 * 2**20),
        cost_estimate=pl.CostEstimate(
            flops=6_000_000_000, bytes_accessed=10_000_000, transcendentals=4_000_000
        ),
    )(sched, *q, *g, *stats, *kv)


def total(*arrays):
    return functools.reduce(lambda a, b: a + b, [a.astype(jnp.float32) for a in arrays])


def shards(queries, out_grad, outputs, lse, kv_pair, span_order, doc_start):
    rows, width = queries.shape
    ctx, head = lax.axis_index("ctx"), lax.axis_index("head")
    core, x = ctx % 2, (ctx // 2) % 4
    y = (head % 2) * 2 + ctx // 8

    kv = {(0, 0): kv_pair[0]}
    kv[1, 0] = move(kv[0, 0], 1, 0)
    kv[3, 0] = move(kv[0, 0], -1, 0)
    kv[2, 0] = move(kv[1, 0], 1, 0)
    for a in (0, 1, 3, 2):
        kv[a, 1] = move(kv[a, 0], 0, 1)
        kv[a, 3] = move(kv[a, 0], 0, -1)
    for a in (0, 1):
        kv[a, 2] = move(kv[a, 1], 0, 1)
    for a in (3, 2):
        kv[a, 2] = move(kv[a, 3], 0, -1)

    q_other, g_other = other_core(queries), other_core(out_grad)
    product = out_grad.astype(jnp.float32) * outputs.astype(jnp.float32)
    delta = jnp.sum(product.reshape(2, SPAN, HEADS, HEAD_DIM), axis=3)
    delta = delta.transpose(0, 2, 1).reshape(2, FLAT)
    lse2 = (lse * LOG2E).reshape(HEADS, 2, SPAN).transpose(1, 0, 2).reshape(2, FLAT)
    starts = jnp.tile(doc_start.astype(jnp.float32).reshape(2, SPAN), (1, HEADS))
    local = jnp.broadcast_to(
        (jnp.arange(FLAT, dtype=jnp.int32) % SPAN).astype(jnp.float32), (2, FLAT)
    )
    stats = jnp.stack([lse2, delta, starts, local], axis=1)
    stats_other = other_core(stats)

    q_spans = jnp.concatenate(
        [
            lax.dynamic_slice_in_dim(span_order, 2 * ctx, 2),
            lax.dynamic_slice_in_dim(span_order, 2 * (ctx ^ 1), 2),
        ]
    )
    bounds = jnp.concatenate([stats[:, 2], stats_other[:, 2]]).astype(jnp.int32)
    first, last = bounds[:, 0], bounds[:, SPAN - 1]
    k_spans = lax.dynamic_index_in_dim(
        span_order.reshape(8, 2, 2).transpose(1, 0, 2), core, 0, keepdims=False
    ).reshape(16)
    offset_a, offset_b = jnp.arange(16) // 4, jnp.arange(16) % 4
    from_x = (x - jnp.where(core == 0, offset_a, offset_b)) % 4
    from_y = (y - jnp.where(core == 0, offset_b, offset_a)) % 4
    slots = (from_y // 2) * 8 + (from_y % 2) * 4 + from_x
    sched = jnp.concatenate(
        [q_spans, first, last, jnp.zeros((4,), jnp.int32), k_spans, slots]
    ).astype(jnp.int32)

    dq_own, dq_send, d0, d1a, d1b, d2a, d2b, d3a, d3b = local_grads(
        sched,
        (queries, q_other),
        (out_grad, g_other),
        (stats, stats_other),
        [kv[a, b] for a in range(4) for b in range(4)],
    )

    t_a, t_b = move(d2a, 0, -1), move(d2b, 0, 1)
    r1b, r3a = move(d1b, 0, -1), move(d3a, 0, 1)
    dq_got = other_core(dq_send)
    r1a = move(total(d1a, t_a).astype(jnp.bfloat16), 0, -1)
    r3b = move(total(d3b, t_b).astype(jnp.bfloat16), 0, 1)
    near = total(d0[:2], r1a, r3a)
    far = total(d0[2:], r1b, r3b)
    t = move(far[0].astype(jnp.bfloat16), -1, 0)
    r_up = move(far[1].astype(jnp.bfloat16), 1, 0)
    r_down = move((near[1] + t.astype(jnp.float32)).astype(jnp.bfloat16), -1, 0)
    kept = near[0] + r_up.astype(jnp.float32) + r_down.astype(jnp.float32)
    dq = (dq_own + dq_got).astype(jnp.bfloat16)
    return dq, kept[None].astype(jnp.bfloat16)


def solution(mesh):
    return jax.shard_map(
        shards,
        mesh=mesh,
        in_specs=(
            P("ctx", "head"),
            P("ctx", "head"),
            P("ctx", "head"),
            P("head", "ctx"),
            P("head", "ctx", None),
            P(),
            P("ctx"),
        ),
        out_specs=(P("ctx", "head"), P("head", "ctx", None)),
        check_vma=False,
    )
```

```python
import functools
import math

import jax
import jax.numpy as jnp
import numpy as np
from jax import lax
from jax.experimental import pallas as pl
from jax.experimental.pallas import tpu as pltpu
from jax.sharding import PartitionSpec as P

HEAD_DIM = 128
SPAN = 192
HEADS = 4
FLAT = HEADS * SPAN
LOG2E = math.log2(math.e)
SCALE = 1.0 / math.sqrt(HEAD_DIM)
AXES = ("ctx", "head")
NT = (((1,), (1,)), ((), ()))


def device_index(x, y, core, z):
    ctx = (y % 2) * 8 + x * 2 + core
    head = z * 2 + y // 2
    return ctx * 16 + head


def places():
    return [(x, y, c, z) for z in range(8) for y in range(4) for x in range(4) for c in range(2)]


STEPS = (
    (("A", 1), ("A", 3), ("B", 1), ("B", 3)),
    (("A", 3), ("A", 1), ("B", 3), ("B", 1)),
)


def reached(x, y, core, steps):
    for axis, bits in steps:
        if (axis == "A") == (core == 0):
            x ^= bits
        else:
            y ^= bits
    return x, y


def swap(block, step):
    pairs = []
    for x, y, core, z in places():
        to_x, to_y = reached(x, y, core, [step])
        pairs.append((device_index(x, y, core, z), device_index(to_x, to_y, core, z)))
    return lax.ppermute(block, AXES, pairs)


def other_core(block):
    return lax.ppermute(block, "ctx", [(i, i ^ 1) for i in range(16)])


def layout_table():
    table = np.zeros((256, 88), np.int32)
    for x, y, core, z in places():
        row = table[device_index(x, y, core, z)]
        ctx = (y % 2) * 8 + x * 2 + core
        row[0:4] = [2 * ctx, 2 * ctx + 1, 2 * (ctx ^ 1), 2 * (ctx ^ 1) + 1]
        for half in range(2):
            for e in range(16):
                steps = [STEPS[half][k] for k in range(4) if e >> k & 1]
                from_x, from_y = reached(x, y, core, steps)
                source = (from_y % 2) * 8 + from_x * 2 + core
                unit = (source // 2) * 2 + half
                row[8 + unit] = 2 * source + half
                row[(24 if from_y < 2 else 40) + unit] = half * 16 + e
                row[56 + half * 16 + e] = from_y < 2
    return table


def grads_kernel(table, spans, *refs):
    q_refs, g_refs, stat_refs, kv_refs = refs[0:2], refs[2:4], refs[4:6], refs[6:10]
    dq_refs, send_refs, keep_refs = refs[10:12], refs[12:14], refs[14:16]
    q_flat, g_flat, stat, kv_all, key_t, dq_t, dkv, first, last = refs[16:]

    for side in range(2):
        for half in range(2):
            qs = 2 * side + half
            rows = pl.ds(half * SPAN, SPAN)
            for h in range(HEADS):
                cols = pl.ds(h * HEAD_DIM, HEAD_DIM)
                out = pl.ds(h * SPAN, SPAN)
                q_flat[qs, out, :] = q_refs[side][rows, cols]
                g_flat[qs, out, :] = g_refs[side][rows, cols]
            stat[qs] = stat_refs[side][half]
            starts = stat_refs[side][half, 2:3, 0:SPAN].astype(jnp.int32)
            first[qs] = jnp.min(starts)
            last[qs] = jnp.max(starts)
    for n in range(4):
        kv_all[pl.ds(8 * n, 8)] = kv_refs[n][...]
    dq_t[...] = jnp.zeros_like(dq_t)
    dkv[...] = jnp.zeros_like(dkv)

    @pl.loop(0, 16)
    def _(ks):
        sk = spans[table[8 + ks]]
        at_k, at_v = table[24 + ks], table[40 + ks]
        key_t[...] = kv_all[at_k].T

        def pair(qs, sq, masked):
            key, value, q, g = kv_all[at_k], kv_all[at_v], q_flat[qs], g_flat[qs]
            lse, delta = stat[qs, 0:1, :], stat[qs, 1:2, :]
            s = lax.dot_general(key, q, NT, preferred_element_type=jnp.float32)
            p = jnp.exp2(s * (SCALE * LOG2E) - lse)
            if masked:
                k_pos = lax.broadcasted_iota(jnp.int32, (SPAN, FLAT), 0) + sk * SPAN
                q_pos = stat[qs, 3:4, :].astype(jnp.int32) + sq * SPAN
                start = stat[qs, 2:3, :].astype(jnp.int32)
                p = jnp.where((k_pos <= q_pos) & (k_pos >= start), p, 0.0)
            p_low = p.astype(jnp.bfloat16)
            dkv[at_v] += jnp.dot(p_low, g, preferred_element_type=jnp.float32)
            dp = lax.dot_general(value, g, NT, preferred_element_type=jnp.float32)
            ds = (p * (dp - delta)).astype(jnp.bfloat16)
            dkv[at_k] += jnp.dot(ds, q, preferred_element_type=jnp.float32)
            dq_t[qs] += jnp.dot(key_t[...], ds, preferred_element_type=jnp.float32)

        @pl.loop(0, 4)
        def _(qs):
            sq = spans[table[qs]]
            active = (sk <= sq) & (sk * SPAN + (SPAN - 1) >= first[qs])
            full = (sk < sq) & (sk * SPAN >= last[qs])

            @pl.when(full)
            def _():
                pair(qs, sq, False)

            @pl.when(active & jnp.logical_not(full))
            def _():
                pair(qs, sq, True)

    for side in range(2):
        for half in range(2):
            flat = dq_t[2 * side + half].T * SCALE
            for h in range(HEADS):
                dq_refs[side][pl.ds(half * SPAN, SPAN), pl.ds(h * HEAD_DIM, HEAD_DIM)] = flat[
                    h * SPAN : (h + 1) * SPAN, :
                ]
    for half in range(2):

        @pl.loop(0, 8)
        def _(e):
            for n, ref in ((0, keep_refs[half]), (8, send_refs[half])):
                slot = half * 16 + n + e
                factor = jnp.where(table[56 + slot] == 1, jnp.float32(SCALE), jnp.float32(1.0))
                ref[e] = (dkv[slot] * factor).astype(ref.dtype)


def local_grads(table, spans, q, g, stats, kv):
    rows, width = q[0].shape
    vmem = pl.BlockSpec(memory_space=pltpu.VMEM)
    smem = pl.BlockSpec(memory_space=pltpu.SMEM)
    blocks = (8, SPAN, HEAD_DIM)
    dq = jax.ShapeDtypeStruct((rows, width), jnp.float32)
    send = jax.ShapeDtypeStruct(blocks, jnp.bfloat16)
    keep = jax.ShapeDtypeStruct(blocks, jnp.float32)
    out = pl.pallas_call(
        grads_kernel,
        out_shape=(dq, dq, send, send, keep, keep),
        in_specs=[smem] * 2 + [vmem] * 10,
        out_specs=(vmem,) * 6,
        scratch_shapes=[
            pltpu.VMEM((4, FLAT, HEAD_DIM), jnp.bfloat16),
            pltpu.VMEM((4, FLAT, HEAD_DIM), jnp.bfloat16),
            pltpu.VMEM((4, 4, FLAT), jnp.float32),
            pltpu.VMEM((32, SPAN, HEAD_DIM), jnp.bfloat16),
            pltpu.VMEM((HEAD_DIM, SPAN), jnp.bfloat16),
            pltpu.VMEM((4, HEAD_DIM, FLAT), jnp.float32),
            pltpu.VMEM((32, SPAN, HEAD_DIM), jnp.float32),
            pltpu.SMEM((4,), jnp.int32),
            pltpu.SMEM((4,), jnp.int32),
        ],
        compiler_params=pltpu.CompilerParams(vmem_limit_bytes=48 * 2**20),
        cost_estimate=pl.CostEstimate(
            flops=6_000_000_000, bytes_accessed=10_000_000, transcendentals=4_000_000
        ),
    )(table, spans, *q, *g, *stats, *kv)
    return out[0:2], out[2:4], out[4:6]


def total(*arrays):
    return functools.reduce(lambda a, b: a + b, [a.astype(jnp.float32) for a in arrays])


def shards(queries, out_grad, outputs, lse, kv_pair, span_order, doc_start):
    rows, width = queries.shape
    mine = lax.axis_index("ctx") * 16 + lax.axis_index("head")
    table = lax.dynamic_index_in_dim(jnp.asarray(layout_table()), mine, 0, keepdims=False)

    own = kv_pair.reshape(2, 1, SPAN, HEAD_DIM)
    held = [own[0], own[1]]
    for k in range(4):
        got = [swap(held[half], STEPS[half][k]) for half in range(2)]
        if k < 3:
            held = [jnp.concatenate([held[half], got[half]]) for half in range(2)]

    q_other, g_other = other_core(queries), other_core(out_grad)
    product = out_grad.astype(jnp.float32) * outputs.astype(jnp.float32)
    delta = jnp.sum(product.reshape(2, SPAN, HEADS, HEAD_DIM), axis=3)
    delta = delta.transpose(0, 2, 1).reshape(2, FLAT)
    lse2 = (lse * LOG2E).reshape(HEADS, 2, SPAN).transpose(1, 0, 2).reshape(2, FLAT)
    starts = jnp.tile(doc_start.astype(jnp.float32).reshape(2, SPAN), (1, HEADS))
    local = jnp.broadcast_to(
        (jnp.arange(FLAT, dtype=jnp.int32) % SPAN).astype(jnp.float32), (2, FLAT)
    )
    stats = jnp.stack([lse2, delta, starts, local], axis=1)
    stats_other = other_core(stats)

    dq, send, keep = local_grads(
        table,
        span_order,
        (queries, q_other),
        (out_grad, g_other),
        (stats, stats_other),
        (held[0], got[0], held[1], got[1]),
    )

    got = [[swap(send[half], STEPS[half][3])] for half in range(2)]
    dq_got = other_core(dq[1])
    for k in (2, 1, 0):
        n = 2**k
        for half in range(2):
            part = total(keep[half][n : 2 * n], *[r[n : 2 * n] for r in got[half]])
            got[half].append(swap(part.astype(jnp.bfloat16), STEPS[half][k]))
    kept = jnp.concatenate([total(keep[half][0:1], *[r[0:1] for r in got[half]]) for half in range(2)])
    return (dq[0] + dq_got).astype(jnp.bfloat16), kept.reshape(1, rows, HEAD_DIM).astype(jnp.bfloat16)


def solution(mesh):
    return jax.shard_map(
        shards,
        mesh=mesh,
        in_specs=(
            P("ctx", "head"),
            P("ctx", "head"),
            P("ctx", "head"),
            P("head", "ctx"),
            P("head", "ctx", None),
            P(),
            P("ctx"),
        ),
        out_specs=(P("ctx", "head"), P("head", "ctx", None)),
        check_vma=False,
    )
```

```python
import functools
import math

import jax
import jax.numpy as jnp
import numpy as np
from jax import lax
from jax.experimental import pallas as pl
from jax.experimental.pallas import tpu as pltpu
from jax.sharding import PartitionSpec as P

HEAD_DIM = 128
SPAN = 192
HEADS = 4
FLAT = HEADS * SPAN
LOG2E = math.log2(math.e)
SCALE = 1.0 / math.sqrt(HEAD_DIM)
AXES = ("ctx", "head")
NT = (((1,), (1,)), ((), ()))


def device_index(x, y, core, z):
    ctx = (y % 2) * 8 + x * 2 + core
    head = z * 2 + y // 2
    return ctx * 16 + head


def places():
    return [(x, y, c, z) for z in range(8) for y in range(4) for x in range(4) for c in range(2)]


def shifted(x, y, core, step_a, step_b):
    dx, dy = (step_a, step_b) if core == 0 else (step_b, step_a)
    return (x + dx) % 4, (y + dy) % 4


def move(block, step_a, step_b):
    pairs = []
    for x, y, core, z in places():
        to_x, to_y = shifted(x, y, core, step_a, step_b)
        pairs.append((device_index(x, y, core, z), device_index(to_x, to_y, core, z)))
    return lax.ppermute(block, AXES, pairs)


def other_core(block):
    return lax.ppermute(block, "ctx", [(i, i ^ 1) for i in range(16)])


BLOCK_B = (0, 1, 3, 2)


def layout_table():
    table = np.zeros((256, 72), np.int32)
    for x, y, core, z in places():
        row = table[device_index(x, y, core, z)]
        ctx = (y % 2) * 8 + x * 2 + core
        row[0:4] = [2 * ctx, 2 * ctx + 1, 2 * (ctx ^ 1), 2 * (ctx ^ 1) + 1]
        for n in range(16):
            from_x, from_y = shifted(x, y, core, -(n % 4), -BLOCK_B[n // 4])
            source = (from_y % 2) * 8 + from_x * 2 + core
            for half in range(2):
                unit = (source // 2) * 2 + half
                row[8 + unit] = 2 * source + half
                row[(24 if from_y < 2 else 40) + unit] = 2 * n + half
            row[56 + n] = from_y < 2
    return table


def stats_kernel(g_ref, o_ref, lse_ref, start_ref, out_ref):
    for half in range(2):
        rows = slice(half * SPAN, half * SPAN + SPAN)
        delta = []
        for h in range(HEADS):
            cols = slice(h * HEAD_DIM, h * HEAD_DIM + HEAD_DIM)
            product = g_ref[rows, cols].astype(jnp.float32) * o_ref[rows, cols].astype(jnp.float32)
            delta.append(jnp.sum(product.T, axis=0, keepdims=True))
        out_ref[half, 0:1, :] = jnp.concatenate(
            [lse_ref[h : h + 1, rows] * LOG2E for h in range(HEADS)], axis=1
        )
        out_ref[half, 1:2, :] = jnp.concatenate(delta, axis=1)
        out_ref[half, 2:3, :] = jnp.concatenate(
            [start_ref[:, rows].astype(jnp.float32)] * HEADS, axis=1
        )
        out_ref[half, 3:4, :] = jnp.concatenate(
            [lax.broadcasted_iota(jnp.int32, (1, SPAN), 1).astype(jnp.float32)] * HEADS, axis=1
        )


def row_stats(out_grad, outputs, lse, doc_start):
    return pl.pallas_call(
        stats_kernel,
        out_shape=jax.ShapeDtypeStruct((2, 4, FLAT), jnp.float32),
        cost_estimate=pl.CostEstimate(flops=400_000, bytes_accessed=800_000, transcendentals=0),
    )(out_grad, outputs, lse, doc_start.reshape(1, -1))


def grads_kernel(table, spans, *refs):
    q_refs, g_refs, stat_refs, kv_refs = refs[0:2], refs[2:4], refs[4:6], refs[6:11]
    dq_refs, d0_ref, d1_ref, d3_ref, d2_refs = refs[11:13], refs[13], refs[14], refs[15], refs[16:18]
    q_flat, g_flat, stat, kv_all, dq_t, dkv, sk_list, met = refs[18:]

    for u in range(16):
        sk_list[u] = spans[table[8 + u]]
    for side in range(2):
        for half in range(2):
            qs = 2 * side + half
            rows = pl.ds(half * SPAN, SPAN)
            for h in range(HEADS):
                cols = pl.ds(h * HEAD_DIM, HEAD_DIM)
                out = pl.ds(h * SPAN, SPAN)
                q_flat[qs, out, :] = q_refs[side][rows, cols]
                g_flat[qs, out, :] = g_refs[side][rows, cols]
            stat[qs] = stat_refs[side][half]
    at = 0
    for ref in kv_refs:
        for n in range(ref.shape[0]):
            kv_all[at] = ref[n, 0:SPAN]
            kv_all[at + 1] = ref[n, SPAN : 2 * SPAN]
            at += 2
    dq_t[...] = jnp.zeros_like(dq_t)
    dkv[...] = jnp.zeros_like(dkv)

    @pl.loop(0, 4)
    def _(qs):
        sq = spans[table[qs]]
        first = jnp.min(stat[qs, 2:3, 0:SPAN].astype(jnp.int32))
        count = jnp.int32(0)
        for u in range(16):
            met[count] = u
            meets = (sk_list[u] <= sq) & (sk_list[u] * SPAN + (SPAN - 1) >= first)
            count = count + meets.astype(jnp.int32)

        def stack(base, size):
            units = [met[base + j] for j in range(size)]
            at_k = [table[24 + u] for u in units]
            at_v = [table[40 + u] for u in units]
            key = jnp.concatenate([kv_all[n] for n in at_k], axis=0)
            value = jnp.concatenate([kv_all[n] for n in at_v], axis=0)
            q, g = q_flat[qs], g_flat[qs]
            lse, delta = stat[qs, 0:1, :], stat[qs, 1:2, :]
            start = stat[qs, 2:3, :].astype(jnp.int32)
            q_pos = stat[qs, 3:4, :].astype(jnp.int32) + sq * SPAN
            s = lax.dot_general(key, q, NT, preferred_element_type=jnp.float32)
            dp = lax.dot_general(value, g, NT, preferred_element_type=jnp.float32)
            p = jnp.exp2(s * (SCALE * LOG2E) - lse)
            local = lax.broadcasted_iota(jnp.int32, (SPAN, FLAT), 0)
            masked = []
            for j, u in enumerate(units):
                shift = sk_list[u] * SPAN
                allowed = (local <= q_pos - shift) & (local >= start - shift)
                masked.append(jnp.where(allowed, p[j * SPAN : (j + 1) * SPAN], 0.0))
            p = jnp.concatenate(masked, axis=0)
            ds = (p * (dp - delta)).astype(jnp.bfloat16)
            dv = jnp.dot(p.astype(jnp.bfloat16), g, preferred_element_type=jnp.float32)
            dk = jnp.dot(ds, q, preferred_element_type=jnp.float32)
            for j in range(size):
                dkv[at_v[j]] += dv[j * SPAN : (j + 1) * SPAN]
                dkv[at_k[j]] += dk[j * SPAN : (j + 1) * SPAN]
            dq_t[qs] += jnp.dot(key.T, ds, preferred_element_type=jnp.float32)

        @pl.loop(0, count // 4)
        def _(i):
            stack(4 * i, 4)

        @pl.when(count % 4 >= 2)
        def _():
            stack(count // 4 * 4, 2)

        @pl.when(count % 2 == 1)
        def _():
            stack(count - 1, 1)

    for side in range(2):
        for half in range(2):
            flat = dq_t[2 * side + half].T * SCALE
            for h in range(HEADS):
                dq_refs[side][pl.ds(half * SPAN, SPAN), pl.ds(h * HEAD_DIM, HEAD_DIM)] = flat[
                    h * SPAN : (h + 1) * SPAN, :
                ]

    at = 0
    for ref in (d0_ref, d1_ref, d3_ref, *d2_refs):
        for n in range(ref.shape[0]):
            factor = jnp.where(table[56 + at] == 1, jnp.float32(SCALE), jnp.float32(1.0))
            for half in range(2):
                ref[n, half * SPAN : (half + 1) * SPAN] = (dkv[2 * at + half] * factor).astype(ref.dtype)
            at += 1


def local_grads(table, spans, q, g, stats, kv):
    rows, width = q[0].shape
    vmem = pl.BlockSpec(memory_space=pltpu.VMEM)
    smem = pl.BlockSpec(memory_space=pltpu.SMEM)
    dq = jax.ShapeDtypeStruct((rows, width), jnp.float32)
    four = jax.ShapeDtypeStruct((4, rows, HEAD_DIM), jnp.float32)
    two = jax.ShapeDtypeStruct((2, rows, HEAD_DIM), jnp.bfloat16)
    return pl.pallas_call(
        grads_kernel,
        out_shape=(dq, dq, four, four, four, two, two),
        in_specs=[smem] * 2 + [vmem] * 11,
        out_specs=(vmem,) * 7,
        scratch_shapes=[
            pltpu.VMEM((4, FLAT, HEAD_DIM), jnp.bfloat16),
            pltpu.VMEM((4, FLAT, HEAD_DIM), jnp.bfloat16),
            pltpu.VMEM((4, 4, FLAT), jnp.float32),
            pltpu.VMEM((32, SPAN, HEAD_DIM), jnp.bfloat16),
            pltpu.VMEM((4, HEAD_DIM, FLAT), jnp.float32),
            pltpu.VMEM((32, SPAN, HEAD_DIM), jnp.float32),
            pltpu.SMEM((16,), jnp.int32),
            pltpu.SMEM((17,), jnp.int32),
        ],
        compiler_params=pltpu.CompilerParams(vmem_limit_bytes=48 * 2**20),
        cost_estimate=pl.CostEstimate(
            flops=6_000_000_000, bytes_accessed=10_000_000, transcendentals=4_000_000
        ),
    )(table, spans, *q, *g, *stats, *kv)


def total(*arrays):
    return functools.reduce(lambda a, b: a + b, [a.astype(jnp.float32) for a in arrays])


def shards(queries, out_grad, outputs, lse, kv_pair, span_order, doc_start):
    rows, width = queries.shape
    mine = lax.axis_index("ctx") * 16 + lax.axis_index("head")
    table = lax.dynamic_index_in_dim(jnp.asarray(layout_table()), mine, 0, keepdims=False)

    stats = row_stats(out_grad, outputs, lse, doc_start)
    stats_other = other_core(stats)
    q_other, g_other = other_core(queries), other_core(out_grad)

    ring = [kv_pair[0], move(kv_pair[0], 1, 0), move(kv_pair[0], 2, 0), move(kv_pair[0], -1, 0)]
    own = jnp.stack(ring)
    up, down = move(own, 0, 1), move(own, 0, -1)
    far = (move(up[:2], 0, 1), move(down[2:], 0, -1))

    dq_own, dq_send, d0, d1, d3, d2_low, d2_high = local_grads(
        table,
        span_order,
        (queries, q_other),
        (out_grad, g_other),
        (stats, stats_other),
        (own, up, down, *far),
    )

    low, high = move(d2_low, 0, -1), move(d2_high, 0, 1)
    dq_got = other_core(dq_send)
    d1 = jnp.concatenate([d1[:2] + low.astype(jnp.float32), d1[2:]])
    d3 = jnp.concatenate([d3[:2], d3[2:] + high.astype(jnp.float32)])
    from_up, from_down = move(d1.astype(jnp.bfloat16), 0, -1), move(d3.astype(jnp.bfloat16), 0, 1)
    ring = total(d0, from_up, from_down)
    sent = ring[1:].astype(jnp.bfloat16)
    dq = (dq_own + dq_got).astype(jnp.bfloat16)
    sent, dq = lax.optimization_barrier((sent, dq))
    kept = total(ring[0], move(sent[1], 2, 0), move(sent[0], -1, 0), move(sent[2], 1, 0))
    return dq, kept[None].astype(jnp.bfloat16)


def solution(mesh):
    return jax.shard_map(
        shards,
        mesh=mesh,
        in_specs=(
            P("ctx", "head"),
            P("ctx", "head"),
            P("ctx", "head"),
            P("head", "ctx"),
            P("head", "ctx", None),
            P(),
            P("ctx"),
        ),
        out_specs=(P("ctx", "head"), P("head", "ctx", None)),
        check_vma=False,
    )
```

```python
import functools
import math

import jax
import jax.numpy as jnp
import numpy as np
from jax import lax
from jax.experimental import pallas as pl
from jax.experimental.pallas import tpu as pltpu
from jax.sharding import PartitionSpec as P

HEAD_DIM = 128
SPAN = 192
HEADS = 4
FLAT = HEADS * SPAN
WIDTH = 88
LOG2E = math.log2(math.e)
SCALE = 1.0 / math.sqrt(HEAD_DIM)
AXES = ("ctx", "head")
NT = (((1,), (1,)), ((), ()))


def device_index(x, y, core, z):
    ctx = (y % 2) * 8 + x * 2 + core
    head = z * 2 + y // 2
    return ctx * 16 + head


def places():
    return [(x, y, c, z) for z in range(8) for y in range(4) for x in range(4) for c in range(2)]


def shifted(x, y, core, step_a, step_b):
    dx, dy = (step_a, step_b) if core == 0 else (step_b, step_a)
    return (x + dx) % 4, (y + dy) % 4


def move(block, step_a, step_b):
    pairs = []
    for x, y, core, z in places():
        to_x, to_y = shifted(x, y, core, step_a, step_b)
        pairs.append((device_index(x, y, core, z), device_index(to_x, to_y, core, z)))
    return lax.ppermute(block, AXES, pairs)


def other_core(block):
    return lax.ppermute(block, "ctx", [(i, i ^ 1) for i in range(16)])


BLOCK_B = (0, 1, 3, 2)


def layout_table():
    table = np.zeros((32, WIDTH), np.int32)
    for x, y, core, z in places():
        ctx = (y % 2) * 8 + x * 2 + core
        row = table[ctx * 2 + y // 2]
        row[0:4] = [2 * ctx, 2 * ctx + 1, 2 * (ctx ^ 1), 2 * (ctx ^ 1) + 1]
        for n in range(16):
            step_b = BLOCK_B[n // 4]
            from_x, from_y = shifted(x, y, core, -(n % 4), -step_b)
            source = (from_y % 2) * 8 + from_x * 2 + core
            for half in range(2):
                unit = (source // 2) * 2 + half
                row[8 + unit] = 2 * source + half
                row[(24 if from_y < 2 else 40) + unit] = 2 * n + half
                if core == 0:
                    row[72 + unit] = 2 if step_b % 2 == 0 else 1 if half == 0 else 3
                elif step_b == 1:
                    row[72 + unit] = 1 if half == 0 else 3
                else:
                    row[72 + unit] = {0: 1, 2: 2, 3: 3}[step_b]
            row[56 + n] = from_y < 2
    return table.reshape(-1)


def prepare_kernel(q_ref, g_ref, o_ref, lse_ref, start_ref, q_flat, g_flat, stat):
    for half in range(2):
        rows = slice(half * SPAN, half * SPAN + SPAN)
        delta = []
        for h in range(HEADS):
            cols = slice(h * HEAD_DIM, h * HEAD_DIM + HEAD_DIM)
            out = slice(h * SPAN, h * SPAN + SPAN)
            q_flat[half, out, :] = q_ref[rows, cols]
            g_flat[half, out, :] = g_ref[rows, cols]
            product = g_ref[rows, cols].astype(jnp.float32) * o_ref[rows, cols].astype(jnp.float32)
            delta.append(jnp.sum(product.T, axis=0, keepdims=True))
        stat[half, 0:1, :] = jnp.concatenate(
            [lse_ref[h : h + 1, rows] * LOG2E for h in range(HEADS)], axis=1
        )
        stat[half, 1:2, :] = jnp.concatenate(delta, axis=1)
        stat[half, 2:3, :] = jnp.concatenate(
            [start_ref[:, rows].astype(jnp.float32)] * HEADS, axis=1
        )
        stat[half, 3:4, :] = jnp.concatenate(
            [lax.broadcasted_iota(jnp.int32, (1, SPAN), 1).astype(jnp.float32)] * HEADS, axis=1
        )


def prepare(queries, out_grad, outputs, lse, doc_start):
    flat = jax.ShapeDtypeStruct((2, FLAT, HEAD_DIM), jnp.bfloat16)
    return pl.pallas_call(
        prepare_kernel,
        out_shape=(flat, flat, jax.ShapeDtypeStruct((2, 4, FLAT), jnp.float32)),
        cost_estimate=pl.CostEstimate(flops=400_000, bytes_accessed=4_000_000, transcendentals=0),
    )(queries, out_grad, outputs, lse, doc_start.reshape(1, -1))


def work(step, table, spans, q_flat, g_flat, stat, kv_all, dq_t, dkv, sk_list, met):
    ctx, head = lax.axis_index("ctx"), lax.axis_index("head")
    base = (ctx * 2 + head % 2) * WIDTH
    for u in range(16):
        sk_list[u] = spans[table[base + 8 + u]]

    @pl.loop(0, 4)
    def _(qs):
        sq = spans[table[base + qs]]
        first = jnp.min(stat[qs, 2:3, 0:SPAN].astype(jnp.int32))
        count = jnp.int32(0)
        for u in range(16):
            met[count] = u
            meets = (sk_list[u] <= sq) & (sk_list[u] * SPAN + (SPAN - 1) >= first)
            meets = meets & (table[base + 72 + u] == step)
            count = count + meets.astype(jnp.int32)

        def stack(begin, size):
            units = [met[begin + j] for j in range(size)]
            at_k = [table[base + 24 + u] for u in units]
            at_v = [table[base + 40 + u] for u in units]
            key = jnp.concatenate([kv_all[n] for n in at_k], axis=0)
            value = jnp.concatenate([kv_all[n] for n in at_v], axis=0)
            q, g = q_flat[qs], g_flat[qs]
            lse, delta = stat[qs, 0:1, :], stat[qs, 1:2, :]
            start = stat[qs, 2:3, :].astype(jnp.int32)
            q_pos = stat[qs, 3:4, :].astype(jnp.int32) + sq * SPAN
            s = lax.dot_general(key, q, NT, preferred_element_type=jnp.float32)
            dp = lax.dot_general(value, g, NT, preferred_element_type=jnp.float32)
            p = jnp.exp2(s * (SCALE * LOG2E) - lse)
            local = lax.broadcasted_iota(jnp.int32, (SPAN, FLAT), 0)
            masked = []
            for j, u in enumerate(units):
                shift = sk_list[u] * SPAN
                allowed = (local <= q_pos - shift) & (local >= start - shift)
                masked.append(jnp.where(allowed, p[j * SPAN : (j + 1) * SPAN], 0.0))
            p = jnp.concatenate(masked, axis=0)
            ds = (p * (dp - delta)).astype(jnp.bfloat16)
            dv = jnp.dot(p.astype(jnp.bfloat16), g, preferred_element_type=jnp.float32)
            dk = jnp.dot(ds, q, preferred_element_type=jnp.float32)
            for j in range(size):
                dkv[at_v[j]] += dv[j * SPAN : (j + 1) * SPAN]
                dkv[at_k[j]] += dk[j * SPAN : (j + 1) * SPAN]
            dq_t[qs] += jnp.dot(key.T, ds, preferred_element_type=jnp.float32)

        @pl.loop(0, count // 4)
        def _(i):
            stack(4 * i, 4)

        @pl.when(count % 4 >= 2)
        def _():
            stack(count // 4 * 4, 2)

        @pl.when(count % 2 == 1)
        def _():
            stack(count - 1, 1)

    return base


def take(kv_all, at, refs):
    for ref in refs:
        for n in range(ref.shape[0]):
            kv_all[at] = ref[n, 0:SPAN]
            kv_all[at + 1] = ref[n, SPAN : 2 * SPAN]
            at += 2


def give(table, base, dkv, at, refs):
    for ref in refs:
        for n in range(ref.shape[0]):
            factor = jnp.where(table[base + 56 + at] == 1, jnp.float32(SCALE), jnp.float32(1.0))
            for half in range(2):
                ref[n, half * SPAN : (half + 1) * SPAN] = (dkv[2 * at + half] * factor).astype(ref.dtype)
            at += 1


def near_kernel(table, spans, q0, q1, g0, g1, s0, s1, own, up, down, *refs):
    q_flat, g_flat, stat, dkv, dq_t, kv_all, _, sk_list, met = refs
    for to, pair in ((q_flat, (q0, q1)), (g_flat, (g0, g1)), (stat, (s0, s1))):
        for side in range(2):
            to[2 * side : 2 * side + 2] = pair[side][...]
    dq_t[...] = jnp.zeros_like(dq_t)
    dkv[...] = jnp.zeros_like(dkv)
    take(kv_all, 0, (own, up, down))
    work(1, table, spans, q_flat, g_flat, stat, kv_all, dq_t, dkv, sk_list, met)


def far_kernel(table, spans, q_flat, g_flat, stat, own, low, high, dq_in, *refs):
    dq_t, e0, d2_low, d2_high, kv_all, dkv, sk_list, met = refs
    dq_t[...] = dq_in[...]
    dkv[0:8] = jnp.zeros_like(dkv[0:8])
    dkv[24:32] = jnp.zeros_like(dkv[24:32])
    take(kv_all, 0, (own,))
    take(kv_all, 24, (low, high))
    base = work(2, table, spans, q_flat, g_flat, stat, kv_all, dq_t, dkv, sk_list, met)
    give(table, base, dkv, 12, (d2_low, d2_high))
    for n in range(8):
        e0[n] = dkv[n]


def rest_kernel(table, spans, q_flat, g_flat, stat, own, up, down, dq_in, dkv_in, e0, *refs):
    dq_own, dq_send, d0, d1, d3, dq_t, kv_all, dkv, sk_list, met = refs
    dq_t[...] = dq_in[...]
    dkv[8:24] = dkv_in[8:24]
    for n in range(8):
        dkv[n] = dkv_in[n] + e0[n]
    take(kv_all, 0, (own, up, down))
    base = work(3, table, spans, q_flat, g_flat, stat, kv_all, dq_t, dkv, sk_list, met)
    for side, ref in enumerate((dq_own, dq_send)):
        for half in range(2):
            flat = dq_t[2 * side + half].T * SCALE
            for h in range(HEADS):
                ref[pl.ds(half * SPAN, SPAN), pl.ds(h * HEAD_DIM, HEAD_DIM)] = flat[
                    h * SPAN : (h + 1) * SPAN, :
                ]
    give(table, base, dkv, 0, (d0, d1, d3))


def call(kernel, inputs, outs, *scratch):
    vmem = pl.BlockSpec(memory_space=pltpu.VMEM)
    smem = pl.BlockSpec(memory_space=pltpu.SMEM)
    return pl.pallas_call(
        kernel,
        out_shape=tuple(jax.ShapeDtypeStruct(*out) for out in outs),
        in_specs=[smem] * 2 + [vmem] * (len(inputs) - 2),
        out_specs=(vmem,) * len(outs),
        scratch_shapes=[
            *scratch,
            pltpu.VMEM((32, SPAN, HEAD_DIM), jnp.bfloat16),
            pltpu.VMEM((32, SPAN, HEAD_DIM), jnp.float32),
            pltpu.SMEM((16,), jnp.int32),
            pltpu.SMEM((17,), jnp.int32),
        ],
        compiler_params=pltpu.CompilerParams(vmem_limit_bytes=36 * 2**20),
        cost_estimate=pl.CostEstimate(
            flops=3_000_000_000, bytes_accessed=12_000_000, transcendentals=1_000_000
        ),
    )(*inputs)


def total(*arrays):
    return functools.reduce(lambda a, b: a + b, [a.astype(jnp.float32) for a in arrays])


def shards(queries, out_grad, outputs, lse, kv_pair, span_order, doc_start):
    rows, width = queries.shape
    table = jnp.asarray(layout_table())

    ring = [kv_pair[0], move(kv_pair[0], 1, 0), move(kv_pair[0], 2, 0), move(kv_pair[0], -1, 0)]
    q, g, stat = prepare(queries, out_grad, outputs, lse, doc_start)
    ring, (q, g, stat) = lax.optimization_barrier((ring, (q, g, stat)))
    own = jnp.stack(ring)
    up, down = move(own, 0, 1), move(own, 0, -1)
    other = [other_core(v) for v in (q, g, stat)]
    up, down, other = lax.optimization_barrier((up, down, other))
    low, high = move(up[:2], 0, 1), move(down[2:], 0, -1)

    f32, b16 = jnp.float32, jnp.bfloat16
    flat, dq_sum = ((4, FLAT, HEAD_DIM), b16), ((4, HEAD_DIM, FLAT), f32)
    four, two = (4, rows, HEAD_DIM), (2, rows, HEAD_DIM)
    *flats, dkv, dq_t = call(
        near_kernel,
        (table, span_order, q, other[0], g, other[1], stat, other[2], own, up, down),
        [flat, flat, ((4, 4, FLAT), f32), ((24, SPAN, HEAD_DIM), f32), dq_sum],
    )
    dq_t, e0, d2_low, d2_high = call(
        far_kernel,
        (table, span_order, *flats, own, low, high, dq_t),
        [dq_sum, ((8, SPAN, HEAD_DIM), f32), (two, b16), (two, b16)],
    )
    low, high = move(d2_low, 0, -1), move(d2_high, 0, 1)
    dq_own, dq_send, d0, d1, d3 = call(
        rest_kernel,
        (table, span_order, *flats, own, up, down, dq_t, dkv, e0),
        [((rows, width), f32), ((rows, width), f32), (four, f32), (four, b16), (four, b16)],
        pltpu.VMEM((4, HEAD_DIM, FLAT), f32),
    )

    dq_got = other_core(dq_send)
    d1 = jnp.concatenate([total(d1[:2], low).astype(b16), d1[2:]])
    d3 = jnp.concatenate([d3[:2], total(d3[2:], high).astype(b16)])
    from_up, from_down = move(d1, 0, -1), move(d3, 0, 1)
    dq = (dq_own + dq_got).astype(b16)
    ring = total(d0, from_up, from_down)
    sent = [ring[n].astype(b16) for n in (1, 2, 3)]
    sent, dq = lax.optimization_barrier((sent, dq))
    kept = total(ring[0], move(sent[0], -1, 0), move(sent[2], 1, 0), move(sent[1], 2, 0))
    return dq, kept[None].astype(b16)


def solution(mesh):
    return jax.shard_map(
        shards,
        mesh=mesh,
        in_specs=(
            P("ctx", "head"),
            P("ctx", "head"),
            P("ctx", "head"),
            P("head", "ctx"),
            P("head", "ctx", None),
            P(),
            P("ctx"),
        ),
        out_specs=(P("ctx", "head"), P("head", "ctx", None)),
        check_vma=False,
    )
```

```python
import functools
import math

import jax
import jax.numpy as jnp
import numpy as np
from jax import lax
from jax.experimental import pallas as pl
from jax.experimental.pallas import tpu as pltpu
from jax.sharding import PartitionSpec as P

HEAD_DIM = 128
SPAN = 192
HEADS = 4
FLAT = HEADS * SPAN
WIDTH = 88
LIST = 49
KINDS = 12 * LIST
LOG2E = math.log2(math.e)
SCALE = 1.0 / math.sqrt(HEAD_DIM)
AXES = ("ctx", "head")
NT = (((1,), (1,)), ((), ()))


def device_index(x, y, core, z):
    ctx = (y % 2) * 8 + x * 2 + core
    head = z * 2 + y // 2
    return ctx * 16 + head


def places():
    return [(x, y, c, z) for z in range(8) for y in range(4) for x in range(4) for c in range(2)]


def shifted(x, y, core, step_a, step_b):
    dx, dy = (step_a, step_b) if core == 0 else (step_b, step_a)
    return (x + dx) % 4, (y + dy) % 4


def move(block, step_a, step_b):
    pairs = []
    for x, y, core, z in places():
        to_x, to_y = shifted(x, y, core, step_a, step_b)
        pairs.append((device_index(x, y, core, z), device_index(to_x, to_y, core, z)))
    return lax.ppermute(block, AXES, pairs)


def other_core(block):
    return lax.ppermute(block, "ctx", [(i, i ^ 1) for i in range(16)])


BLOCK_B = (0, 1, 3, 2)


def layout_table():
    table = np.zeros((32, WIDTH), np.int32)
    for x, y, core, z in places():
        ctx = (y % 2) * 8 + x * 2 + core
        row = table[ctx * 2 + y // 2]
        row[0:4] = [2 * ctx, 2 * ctx + 1, 2 * (ctx ^ 1), 2 * (ctx ^ 1) + 1]
        for n in range(16):
            step_b = BLOCK_B[n // 4]
            from_x, from_y = shifted(x, y, core, -(n % 4), -step_b)
            source = (from_y % 2) * 8 + from_x * 2 + core
            for half in range(2):
                unit = (source // 2) * 2 + half
                row[8 + unit] = 2 * source + half
                row[(24 if from_y < 2 else 40) + unit] = 2 * n + half
                if core == 0:
                    row[72 + unit] = 2 if step_b % 2 == 0 else 1 if half == 0 else 3
                elif step_b == 1:
                    row[72 + unit] = 1 if half == 0 else 3
                else:
                    row[72 + unit] = {0: 1, 2: 2, 3: 3}[step_b]
            row[56 + n] = from_y < 2
    return table.reshape(-1)


def prepare_kernel(q_ref, g_ref, o_ref, lse_ref, start_ref, q_flat, g_flat, stat):
    for half in range(2):
        rows = slice(half * SPAN, half * SPAN + SPAN)
        delta = []
        for h in range(HEADS):
            cols = slice(h * HEAD_DIM, h * HEAD_DIM + HEAD_DIM)
            out = slice(h * SPAN, h * SPAN + SPAN)
            q_flat[half, out, :] = q_ref[rows, cols]
            g_flat[half, out, :] = g_ref[rows, cols]
            product = g_ref[rows, cols].astype(jnp.float32) * o_ref[rows, cols].astype(jnp.float32)
            delta.append(jnp.sum(product.T, axis=0, keepdims=True))
        stat[half, 0:1, :] = jnp.concatenate(
            [lse_ref[h : h + 1, rows] * LOG2E for h in range(HEADS)], axis=1
        )
        stat[half, 1:2, :] = jnp.concatenate(delta, axis=1)
        stat[half, 2:3, :] = jnp.concatenate(
            [start_ref[0:1, rows].astype(jnp.float32)] * HEADS, axis=1
        )
        stat[half, 3:4, :] = jnp.concatenate(
            [lax.broadcasted_iota(jnp.int32, (1, SPAN), 1).astype(jnp.float32)] * HEADS, axis=1
        )


def prepare(queries, out_grad, outputs, lse, doc_start):
    flat = jax.ShapeDtypeStruct((2, FLAT, HEAD_DIM), jnp.bfloat16)
    return pl.pallas_call(
        prepare_kernel,
        out_shape=(flat, flat, jax.ShapeDtypeStruct((2, 4, FLAT), jnp.float32)),
        cost_estimate=pl.CostEstimate(flops=400_000, bytes_accessed=4_000_000, transcendentals=0),
    )(queries, out_grad, outputs, lse, jnp.broadcast_to(doc_start[None], (8, doc_start.shape[0])))


def plan_kernel(table, spans, q0, q1, g0, g1, s0, s1, q_flat, g_flat, stat, plan):
    ctx, head = lax.axis_index("ctx"), lax.axis_index("head")
    base = (ctx * 2 + head % 2) * WIDTH
    for to, pair in ((q_flat, (q0, q1)), (g_flat, (g0, g1)), (stat, (s0, s1))):
        for side in range(2):
            to[2 * side : 2 * side + 2] = pair[side][...]
    first = []
    for qs in range(4):
        starts = (s0, s1)[qs // 2][qs % 2, 2:3, 0:SPAN]
        first.append(jnp.min(starts.astype(jnp.int32)))
    for n in range(12):
        plan[n * LIST] = 0
    for n in range(16):
        plan[KINDS + n] = table[base + 56 + n]
    begin = []
    for qs in range(4):
        begin.append(spans[table[base + qs]] * SPAN)
        plan[KINDS + 16 + qs] = begin[qs]

    @pl.loop(0, 16)
    def _(u):
        k_begin = spans[table[base + 8 + u]] * SPAN
        at_k, at_v = table[base + 24 + u], table[base + 40 + u]
        step = table[base + 72 + u] - 1
        for qs in range(4):
            at = (step * 4 + qs) * LIST
            count = plan[at]
            plan[at + 1 + 3 * count] = at_k
            plan[at + 2 + 3 * count] = at_v
            plan[at + 3 + 3 * count] = k_begin
            meets = (k_begin <= begin[qs]) & (k_begin + (SPAN - 1) >= first[qs])
            plan[at] = count + meets.astype(jnp.int32)


def work(step, plan, q_flat, g_flat, stat, kv_all, dq_t, dkv):
    @pl.loop(0, 4)
    def _(qs):
        at = ((step - 1) * 4 + qs) * LIST
        count = plan[at]
        q_begin = plan[KINDS + 16 + qs]

        def stack(begin, size):
            at_k = [plan[at + 1 + 3 * (begin + j)] for j in range(size)]
            at_v = [plan[at + 2 + 3 * (begin + j)] for j in range(size)]
            k_begin = [plan[at + 3 + 3 * (begin + j)] for j in range(size)]
            key = jnp.concatenate([kv_all[n] for n in at_k], axis=0)
            value = jnp.concatenate([kv_all[n] for n in at_v], axis=0)
            q, g = q_flat[qs], g_flat[qs]
            lse, delta = stat[qs, 0:1, :], stat[qs, 1:2, :]
            start = stat[qs, 2:3, :].astype(jnp.int32)
            q_pos = stat[qs, 3:4, :].astype(jnp.int32) + q_begin
            s = lax.dot_general(key, q, NT, preferred_element_type=jnp.float32)
            dp = lax.dot_general(value, g, NT, preferred_element_type=jnp.float32)
            p = jnp.exp2(s * (SCALE * LOG2E) - lse)
            local = lax.broadcasted_iota(jnp.int32, (SPAN, FLAT), 0)
            masked = []
            for j in range(size):
                allowed = (local <= q_pos - k_begin[j]) & (local >= start - k_begin[j])
                masked.append(jnp.where(allowed, p[j * SPAN : (j + 1) * SPAN], 0.0))
            p = jnp.concatenate(masked, axis=0)
            ds = (p * (dp - delta)).astype(jnp.bfloat16)
            dv = jnp.dot(p.astype(jnp.bfloat16), g, preferred_element_type=jnp.float32)
            dk = jnp.dot(ds, q, preferred_element_type=jnp.float32)
            for j in range(size):
                dkv[at_v[j]] += dv[j * SPAN : (j + 1) * SPAN]
                dkv[at_k[j]] += dk[j * SPAN : (j + 1) * SPAN]
            dq_t[qs] += jnp.dot(key.T, ds, preferred_element_type=jnp.float32)

        @pl.loop(0, count // 4)
        def _(i):
            stack(4 * i, 4)

        @pl.when(count % 4 >= 2)
        def _():
            stack(count // 4 * 4, 2)

        @pl.when(count % 2 == 1)
        def _():
            stack(count - 1, 1)


def take(kv_all, at, refs):
    for ref in refs:
        for n in range(ref.shape[0]):
            kv_all[at] = ref[n, 0:SPAN]
            kv_all[at + 1] = ref[n, SPAN : 2 * SPAN]
            at += 2


def give(plan, dkv, at, refs):
    for ref in refs:
        for n in range(ref.shape[0]):
            factor = jnp.where(plan[KINDS + at] == 1, jnp.float32(SCALE), jnp.float32(1.0))
            for half in range(2):
                ref[n, half * SPAN : (half + 1) * SPAN] = (dkv[2 * at + half] * factor).astype(ref.dtype)
            at += 1


def near_kernel(plan, q_flat, g_flat, stat, own, up, down, dkv, dq_t, kv_all):
    dq_t[...] = jnp.zeros_like(dq_t)
    dkv[...] = jnp.zeros_like(dkv)
    take(kv_all, 0, (own, up, down))
    work(1, plan, q_flat, g_flat, stat, kv_all, dq_t, dkv)


def far_kernel(plan, q_flat, g_flat, stat, own, low, high, dq_in, dq_t, e0, d2_low, d2_high, kv_all, dkv):
    dq_t[...] = dq_in[...]
    dkv[0:8] = jnp.zeros_like(dkv[0:8])
    dkv[24:32] = jnp.zeros_like(dkv[24:32])
    take(kv_all, 0, (own,))
    take(kv_all, 24, (low, high))
    work(2, plan, q_flat, g_flat, stat, kv_all, dq_t, dkv)
    give(plan, dkv, 12, (d2_low, d2_high))
    for n in range(8):
        e0[n] = dkv[n]


def rest_kernel(
    plan, q_flat, g_flat, stat, own, up, down, dq_in, dkv_in, e0, dq_own, dq_send, d0, d1, d3, kv_all, dkv, dq_t
):
    dq_t[...] = dq_in[...]
    dkv[8:24] = dkv_in[8:24]
    for n in range(8):
        dkv[n] = dkv_in[n] + e0[n]
    take(kv_all, 0, (own, up, down))
    work(3, plan, q_flat, g_flat, stat, kv_all, dq_t, dkv)
    give(plan, dkv, 0, (d0, d1, d3))
    dq_own[...] = dq_t[0:2]
    dq_send[...] = dq_t[2:4]


def rows_kernel(dq_own, dq_got, dq):
    for half in range(2):
        flat = ((dq_own[half] + dq_got[half]) * SCALE).T.astype(dq.dtype)
        for h in range(HEADS):
            dq[pl.ds(half * SPAN, SPAN), pl.ds(h * HEAD_DIM, HEAD_DIM)] = flat[
                h * SPAN : (h + 1) * SPAN, :
            ]


def call(kernel, scalars, inputs, outs, scratch=(), scalar_out=None, flops=3_000_000_000):
    vmem = pl.BlockSpec(memory_space=pltpu.VMEM)
    smem = pl.BlockSpec(memory_space=pltpu.SMEM)
    out_specs = [vmem] * len(outs)
    if scalar_out is not None:
        outs, out_specs = [*outs, scalar_out], [*out_specs, smem]
    return pl.pallas_call(
        kernel,
        out_shape=tuple(jax.ShapeDtypeStruct(*out) for out in outs),
        in_specs=[smem] * len(scalars) + [vmem] * len(inputs),
        out_specs=tuple(out_specs),
        scratch_shapes=[pltpu.VMEM(*s) for s in scratch],
        compiler_params=pltpu.CompilerParams(vmem_limit_bytes=36 * 2**20),
        cost_estimate=pl.CostEstimate(
            flops=flops, bytes_accessed=flops // 300, transcendentals=0
        ),
    )(*scalars, *inputs)


def total(*arrays):
    return functools.reduce(lambda a, b: a + b, [a.astype(jnp.float32) for a in arrays])


def shards(queries, out_grad, outputs, lse, kv_pair, span_order, doc_start):
    rows, width = queries.shape
    table = jnp.asarray(layout_table())

    ring = [kv_pair[0], move(kv_pair[0], 1, 0), move(kv_pair[0], 2, 0), move(kv_pair[0], -1, 0)]
    q, g, stat = prepare(queries, out_grad, outputs, lse, doc_start)
    ring, (q, g, stat) = lax.optimization_barrier((ring, (q, g, stat)))
    own = jnp.stack(ring)
    up, down = move(own, 0, 1), move(own, 0, -1)
    other = [other_core(v) for v in (stat, q, g)]

    f32, b16 = jnp.float32, jnp.bfloat16
    flat, dq_sum = ((4, FLAT, HEAD_DIM), b16), ((4, HEAD_DIM, FLAT), f32)
    blocks = ((32, SPAN, HEAD_DIM), b16), ((32, SPAN, HEAD_DIM), f32)
    four, two = (4, rows, HEAD_DIM), (2, rows, HEAD_DIM)
    *flats, plan = call(
        plan_kernel,
        (table, span_order),
        (q, other[1], g, other[2], stat, other[0]),
        [flat, flat, ((4, 4, FLAT), f32)],
        scalar_out=((KINDS + 20,), jnp.int32),
        flops=1_000_000_000,
    )
    up, down, flats, plan = lax.optimization_barrier((up, down, flats, plan))
    low, high = move(up[:2], 0, 1), move(down[2:], 0, -1)

    dkv, dq_t = call(
        near_kernel,
        (plan,),
        (*flats, own, up, down),
        [((24, SPAN, HEAD_DIM), f32), dq_sum],
        blocks[:1],
    )
    dq_t, e0, d2_low, d2_high = call(
        far_kernel,
        (plan,),
        (*flats, own, low, high, dq_t),
        [dq_sum, ((8, SPAN, HEAD_DIM), f32), (two, b16), (two, b16)],
        blocks,
    )
    low, high = move(d2_low, 0, -1), move(d2_high, 0, 1)
    half_sum = ((2, HEAD_DIM, FLAT), f32)
    dq_own, dq_send, d0, d1, d3 = call(
        rest_kernel,
        (plan,),
        (*flats, own, up, down, dq_t, dkv, e0),
        [half_sum, half_sum, (four, f32), (four, b16), (four, b16)],
        (*blocks, dq_sum),
    )

    low, high, d1, d3 = lax.optimization_barrier((low, high, d1, d3))
    d1 = jnp.concatenate([total(d1[:2], low).astype(b16), d1[2:]])
    d3 = jnp.concatenate([d3[:2], total(d3[2:], high).astype(b16)])
    d1, d3, dq_send = lax.optimization_barrier((d1, d3, dq_send))
    from_up, from_down = move(d1, 0, -1), move(d3, 0, 1)
    (dq,) = call(
        rows_kernel,
        (),
        (dq_own, other_core(dq_send)),
        [((rows, width), b16)],
        flops=1_000_000_000,
    )
    from_up, from_down, dq = lax.optimization_barrier((from_up, from_down, dq))
    ring = total(d0, from_up, from_down)
    sent = [ring[n].astype(b16) for n in (1, 2, 3)]
    kept = total(ring[0], move(sent[0], -1, 0), move(sent[2], 1, 0), move(sent[1], 2, 0))
    return dq, kept[None].astype(b16)


def solution(mesh):
    return jax.shard_map(
        shards,
        mesh=mesh,
        in_specs=(
            P("ctx", "head"),
            P("ctx", "head"),
            P("ctx", "head"),
            P("head", "ctx"),
            P("head", "ctx", None),
            P(),
            P("ctx"),
        ),
        out_specs=(P("ctx", "head"), P("head", "ctx", None)),
        check_vma=False,
    )
```

```python
import functools
import math

import jax
import jax.numpy as jnp
import numpy as np
from jax import lax
from jax.experimental import pallas as pl
from jax.experimental.pallas import tpu as pltpu
from jax.sharding import PartitionSpec as P

HEAD_DIM = 128
SPAN = 192
HEADS = 4
FLAT = HEADS * SPAN
WIDTH = 88
LIST = 49
KINDS = 8 * LIST
LOG2E = math.log2(math.e)
SCALE = 1.0 / math.sqrt(HEAD_DIM)
AXES = ("ctx", "head")
NT = (((1,), (1,)), ((), ()))


def device_index(x, y, core, z):
    ctx = (y % 2) * 8 + x * 2 + core
    head = z * 2 + y // 2
    return ctx * 16 + head


def places():
    return [(x, y, c, z) for z in range(8) for y in range(4) for x in range(4) for c in range(2)]


def shifted(x, y, core, step_a, step_b):
    dx, dy = (step_a, step_b) if core == 0 else (step_b, step_a)
    return (x + dx) % 4, (y + dy) % 4


def move(block, step_a, step_b):
    pairs = []
    for x, y, core, z in places():
        to_x, to_y = shifted(x, y, core, step_a, step_b)
        pairs.append((device_index(x, y, core, z), device_index(to_x, to_y, core, z)))
    return lax.ppermute(block, AXES, pairs)


def other_core(block):
    return lax.ppermute(block, "ctx", [(i, i ^ 1) for i in range(16)])


BLOCK_B = (0, 1, 3, 2)


def layout_table():
    table = np.zeros((32, WIDTH), np.int32)
    for x, y, core, z in places():
        ctx = (y % 2) * 8 + x * 2 + core
        row = table[ctx * 2 + y // 2]
        row[0:4] = [2 * ctx, 2 * ctx + 1, 2 * (ctx ^ 1), 2 * (ctx ^ 1) + 1]
        for n in range(16):
            step_b = BLOCK_B[n // 4]
            from_x, from_y = shifted(x, y, core, -(n % 4), -step_b)
            source = (from_y % 2) * 8 + from_x * 2 + core
            for half in range(2):
                unit = (source // 2) * 2 + half
                row[8 + unit] = 2 * source + half
                row[(24 if from_y < 2 else 40) + unit] = 2 * n + half
                row[72 + unit] |= step_b == 2
            row[56 + n] = from_y < 2
    return table.reshape(-1)


def prepare_kernel(q_ref, g_ref, o_ref, lse_ref, start_ref, kv_ref, q_flat, g_flat, stat, kv):
    kv[...] = kv_ref[...]
    for half in range(2):
        rows = slice(half * SPAN, half * SPAN + SPAN)
        delta = []
        for h in range(HEADS):
            cols = slice(h * HEAD_DIM, h * HEAD_DIM + HEAD_DIM)
            out = slice(h * SPAN, h * SPAN + SPAN)
            q_flat[half, out, :] = q_ref[rows, cols]
            g_flat[half, out, :] = g_ref[rows, cols]
            product = g_ref[rows, cols].astype(jnp.float32) * o_ref[rows, cols].astype(jnp.float32)
            delta.append(jnp.sum(product.T, axis=0, keepdims=True))
        stat[half, 0:1, :] = jnp.concatenate(
            [lse_ref[h : h + 1, rows] * LOG2E for h in range(HEADS)], axis=1
        )
        stat[half, 1:2, :] = jnp.concatenate(delta, axis=1)
        stat[half, 2:3, :] = jnp.concatenate(
            [start_ref[0:1, rows].astype(jnp.float32)] * HEADS, axis=1
        )
        stat[half, 3:4, :] = jnp.concatenate(
            [lax.broadcasted_iota(jnp.int32, (1, SPAN), 1).astype(jnp.float32)] * HEADS, axis=1
        )


def plan_kernel(table, spans, q0, q1, g0, g1, s0, s1, q_flat, g_flat, stat, plan):
    ctx, head = lax.axis_index("ctx"), lax.axis_index("head")
    base = (ctx * 2 + head % 2) * WIDTH
    for to, pair in ((q_flat, (q0, q1)), (g_flat, (g0, g1)), (stat, (s0, s1))):
        for side in range(2):
            to[2 * side : 2 * side + 2] = pair[side][...]
    first = []
    for qs in range(4):
        starts = (s0, s1)[qs // 2][qs % 2, 2:3, 0:SPAN]
        first.append(jnp.min(starts.astype(jnp.int32)))
    for n in range(8):
        plan[n * LIST] = 0
    for n in range(16):
        plan[KINDS + n] = table[base + 56 + n]
    begin = []
    for qs in range(4):
        begin.append(spans[table[base + qs]] * SPAN)
        plan[KINDS + 16 + qs] = begin[qs]

    @pl.loop(0, 16)
    def _(u):
        k_begin = spans[table[base + 8 + u]] * SPAN
        at_k, at_v = table[base + 24 + u], table[base + 40 + u]
        far = table[base + 72 + u]
        for qs in range(4):
            at = (far * 4 + qs) * LIST
            count = plan[at]
            plan[at + 1 + 3 * count] = at_k
            plan[at + 2 + 3 * count] = at_v
            plan[at + 3 + 3 * count] = k_begin
            meets = (k_begin <= begin[qs]) & (k_begin + (SPAN - 1) >= first[qs])
            plan[at] = count + meets.astype(jnp.int32)


def work(far, low, high, plan, q_flat, g_flat, stat, kv_all, dq_t, dkv):
    @pl.loop(low, high)
    def _(qs):
        at = (far * 4 + qs) * LIST
        count = plan[at]
        q_begin = plan[KINDS + 16 + qs]

        def stack(begin, size):
            at_k = [plan[at + 1 + 3 * (begin + j)] for j in range(size)]
            at_v = [plan[at + 2 + 3 * (begin + j)] for j in range(size)]
            k_begin = [plan[at + 3 + 3 * (begin + j)] for j in range(size)]
            key = jnp.concatenate([kv_all[n] for n in at_k], axis=0)
            value = jnp.concatenate([kv_all[n] for n in at_v], axis=0)
            q, g = q_flat[qs], g_flat[qs]
            lse, delta = stat[qs, 0:1, :], stat[qs, 1:2, :]
            start = stat[qs, 2:3, :].astype(jnp.int32)
            q_pos = stat[qs, 3:4, :].astype(jnp.int32) + q_begin
            s = lax.dot_general(key, q, NT, preferred_element_type=jnp.float32)
            dp = lax.dot_general(value, g, NT, preferred_element_type=jnp.float32)
            p = jnp.exp2(s * (SCALE * LOG2E) - lse)
            local = lax.broadcasted_iota(jnp.int32, (SPAN, FLAT), 0)
            masked = []
            for j in range(size):
                allowed = (local <= q_pos - k_begin[j]) & (local >= start - k_begin[j])
                masked.append(jnp.where(allowed, p[j * SPAN : (j + 1) * SPAN], 0.0))
            p = jnp.concatenate(masked, axis=0)
            ds = (p * (dp - delta)).astype(jnp.bfloat16)
            dv = jnp.dot(p.astype(jnp.bfloat16), g, preferred_element_type=jnp.float32)
            dk = jnp.dot(ds, q, preferred_element_type=jnp.float32)
            for j in range(size):
                dkv[at_v[j]] += dv[j * SPAN : (j + 1) * SPAN]
                dkv[at_k[j]] += dk[j * SPAN : (j + 1) * SPAN]
            dq_t[qs - low] += jnp.dot(key.T, ds, preferred_element_type=jnp.float32)

        @pl.loop(0, count // 4)
        def _(i):
            stack(4 * i, 4)

        @pl.when(count % 4 >= 2)
        def _():
            stack(count // 4 * 4, 2)

        @pl.when(count % 2 == 1)
        def _():
            stack(count - 1, 1)


def take(kv_all, at, refs):
    for ref in refs:
        for n in range(ref.shape[0]):
            kv_all[at] = ref[n, 0:SPAN]
            kv_all[at + 1] = ref[n, SPAN : 2 * SPAN]
            at += 2


def give(plan, dkv, at, refs):
    for ref in refs:
        for n in range(ref.shape[0]):
            factor = jnp.where(plan[KINDS + at] == 1, jnp.float32(SCALE), jnp.float32(1.0))
            for half in range(2):
                ref[n, half * SPAN : (half + 1) * SPAN] = (dkv[2 * at + half] * factor).astype(ref.dtype)
            at += 1


def own_kernel(plan, q_flat, g_flat, stat, own, up, down, dkv, dq_t, kv_all):
    dq_t[...] = jnp.zeros_like(dq_t)
    dkv[...] = jnp.zeros_like(dkv)
    take(kv_all, 0, (own, up, down))
    work(0, 0, 2, plan, q_flat, g_flat, stat, kv_all, dq_t, dkv)


def far_kernel(plan, q_flat, g_flat, stat, own, low, high, dq_in, dq_t, e0, d2_low, d2_high, kv_all, dkv):
    dq_t[0:2] = dq_in[...]
    dq_t[2:4] = jnp.zeros_like(dq_t[2:4])
    dkv[0:8] = jnp.zeros_like(dkv[0:8])
    dkv[24:32] = jnp.zeros_like(dkv[24:32])
    take(kv_all, 0, (own,))
    take(kv_all, 24, (low, high))
    work(1, 0, 4, plan, q_flat, g_flat, stat, kv_all, dq_t, dkv)
    give(plan, dkv, 12, (d2_low, d2_high))
    for n in range(8):
        e0[n] = dkv[n]


def other_kernel(
    plan, q_flat, g_flat, stat, own, up, down, dq_in, dkv_in, e0, dq_t, d0, d1, d3, kv_all, dkv
):
    dq_t[...] = dq_in[2:4]
    dkv[8:24] = dkv_in[8:24]
    for n in range(8):
        dkv[n] = dkv_in[n] + e0[n]
    take(kv_all, 0, (own, up, down))
    work(0, 2, 4, plan, q_flat, g_flat, stat, kv_all, dq_t, dkv)
    give(plan, dkv, 0, (d0, d1, d3))


def rows_kernel(dq_own, dq_got, dq):
    for half in range(2):
        flat = ((dq_own[half] + dq_got[half]) * SCALE).T.astype(dq.dtype)
        for h in range(HEADS):
            dq[pl.ds(half * SPAN, SPAN), pl.ds(h * HEAD_DIM, HEAD_DIM)] = flat[
                h * SPAN : (h + 1) * SPAN, :
            ]


def call(kernel, scalars, inputs, outs, scratch=(), scalar_out=None, flops=3_000_000_000):
    vmem = pl.BlockSpec(memory_space=pltpu.VMEM)
    smem = pl.BlockSpec(memory_space=pltpu.SMEM)
    out_specs = [vmem] * len(outs)
    if scalar_out is not None:
        outs, out_specs = [*outs, scalar_out], [*out_specs, smem]
    return pl.pallas_call(
        kernel,
        out_shape=tuple(jax.ShapeDtypeStruct(*out) for out in outs),
        in_specs=[smem] * len(scalars) + [vmem] * len(inputs),
        out_specs=tuple(out_specs),
        scratch_shapes=[pltpu.VMEM(*s) for s in scratch],
        compiler_params=pltpu.CompilerParams(vmem_limit_bytes=36 * 2**20),
        cost_estimate=pl.CostEstimate(
            flops=flops, bytes_accessed=flops // 300, transcendentals=0
        ),
    )(*scalars, *inputs)


def total(*arrays):
    return functools.reduce(lambda a, b: a + b, [a.astype(jnp.float32) for a in arrays])


def shards(queries, out_grad, outputs, lse, kv_pair, span_order, doc_start):
    rows, width = queries.shape
    table = jnp.asarray(layout_table())

    f32, b16 = jnp.float32, jnp.bfloat16
    pair, flat = ((2, FLAT, HEAD_DIM), b16), ((4, FLAT, HEAD_DIM), b16)
    half_sum, dq_sum = ((2, HEAD_DIM, FLAT), f32), ((4, HEAD_DIM, FLAT), f32)
    blocks = ((32, SPAN, HEAD_DIM), b16), ((32, SPAN, HEAD_DIM), f32)
    four, two = (4, rows, HEAD_DIM), (2, rows, HEAD_DIM)
    ring = [move(kv_pair[0], 1, 0), move(kv_pair[0], 2, 0), move(kv_pair[0], -1, 0)]
    q, g, stat, shard = call(
        prepare_kernel,
        (),
        (queries, out_grad, outputs, lse, jnp.broadcast_to(doc_start[None], (8, rows)), kv_pair[0]),
        [pair, pair, ((2, 4, FLAT), f32), ((rows, HEAD_DIM), b16)],
        flops=1_000_000_000,
    )
    other = [other_core(v) for v in (stat, q, g)]
    ring, shard, other = lax.optimization_barrier((ring, shard, other))
    own = jnp.stack([shard, *ring])
    up, down = move(own, 0, 1), move(own, 0, -1)
    *flats, plan = call(
        plan_kernel,
        (table, span_order),
        (q, other[1], g, other[2], stat, other[0]),
        [flat, flat, ((4, 4, FLAT), f32)],
        scalar_out=((KINDS + 20,), jnp.int32),
        flops=1_000_000_000,
    )
    up, down, flats, plan = lax.optimization_barrier((up, down, flats, plan))
    low, high = move(up[:2], 0, 1), move(down[2:], 0, -1)

    dkv, dq_own = call(
        own_kernel,
        (plan,),
        (*flats, own, up, down),
        [((24, SPAN, HEAD_DIM), f32), half_sum],
        blocks[:1],
    )
    dq_own, e0, d2_low, d2_high = call(
        far_kernel,
        (plan,),
        (*flats, own, low, high, dq_own),
        [dq_sum, ((8, SPAN, HEAD_DIM), f32), (two, b16), (two, b16)],
        blocks,
    )
    low, high = move(d2_low, 0, -1), move(d2_high, 0, 1)
    dq_send, d0, d1, d3 = call(
        other_kernel,
        (plan,),
        (*flats, own, up, down, dq_own, dkv, e0),
        [half_sum, (four, f32), (four, b16), (four, b16)],
        blocks,
    )

    low, high, d1, d3 = lax.optimization_barrier((low, high, d1, d3))
    d1 = jnp.concatenate([total(d1[:2], low).astype(b16), d1[2:]])
    d3 = jnp.concatenate([d3[:2], total(d3[2:], high).astype(b16)])
    d1, d3, dq_send = lax.optimization_barrier((d1, d3, dq_send))
    from_up, from_down = move(d1, 0, -1), move(d3, 0, 1)
    (dq,) = call(
        rows_kernel,
        (),
        (dq_own, other_core(dq_send)),
        [((rows, width), b16)],
        flops=1_000_000_000,
    )
    from_up, from_down, dq = lax.optimization_barrier((from_up, from_down, dq))
    ring = total(d0, from_up, from_down)
    sent = [ring[n].astype(b16) for n in (1, 2, 3)]
    kept = total(ring[0], move(sent[0], -1, 0), move(sent[2], 1, 0), move(sent[1], 2, 0))
    return dq, kept[None].astype(b16)


def solution(mesh):
    return jax.shard_map(
        shards,
        mesh=mesh,
        in_specs=(
            P("ctx", "head"),
            P("ctx", "head"),
            P("ctx", "head"),
            P("head", "ctx"),
            P("head", "ctx", None),
            P(),
            P("ctx"),
        ),
        out_specs=(P("ctx", "head"), P("head", "ctx", None)),
        check_vma=False,
    )
```

```python
import functools
import math

import jax
import jax.numpy as jnp
import numpy as np
from jax import lax
from jax.experimental import pallas as pl
from jax.experimental.pallas import tpu as pltpu
from jax.sharding import PartitionSpec as P

HEAD_DIM = 128
SPAN = 192
HEADS = 4
FLAT = HEADS * SPAN
WIDTH = 88
LIST = 49
KINDS = 8 * LIST
LOG2E = math.log2(math.e)
SCALE = 1.0 / math.sqrt(HEAD_DIM)
AXES = ("ctx", "head")
NT = (((1,), (1,)), ((), ()))


def device_index(x, y, core, z):
    ctx = (y % 2) * 8 + x * 2 + core
    head = z * 2 + y // 2
    return ctx * 16 + head


def places():
    return [(x, y, c, z) for z in range(8) for y in range(4) for x in range(4) for c in range(2)]


def shifted(x, y, core, step_a, step_b):
    dx, dy = (step_a, step_b) if core == 0 else (step_b, step_a)
    return (x + dx) % 4, (y + dy) % 4


def move(block, step_a, step_b):
    pairs = []
    for x, y, core, z in places():
        to_x, to_y = shifted(x, y, core, step_a, step_b)
        pairs.append((device_index(x, y, core, z), device_index(to_x, to_y, core, z)))
    return lax.ppermute(block, AXES, pairs)


def other_core(block):
    return lax.ppermute(block, "ctx", [(i, i ^ 1) for i in range(16)])


BLOCK_B = (0, 1, 3, 2)


def layout_table():
    table = np.zeros((32, WIDTH), np.int32)
    for x, y, core, z in places():
        ctx = (y % 2) * 8 + x * 2 + core
        row = table[ctx * 2 + y // 2]
        row[0:4] = [2 * ctx, 2 * ctx + 1, 2 * (ctx ^ 1), 2 * (ctx ^ 1) + 1]
        for n in range(16):
            step_b = BLOCK_B[n // 4]
            from_x, from_y = shifted(x, y, core, -(n % 4), -step_b)
            source = (from_y % 2) * 8 + from_x * 2 + core
            for half in range(2):
                unit = (source // 2) * 2 + half
                row[8 + unit] = 2 * source + half
                row[(24 if from_y < 2 else 40) + unit] = 2 * n + half
                row[72 + unit] |= step_b == 2
            row[56 + n] = from_y < 2
    return table.reshape(-1)


def prepare_kernel(q_ref, g_ref, o_ref, lse_ref, start_ref, kv_ref, q_flat, g_flat, stat, kv):
    kv[...] = kv_ref[...]
    for half in range(2):
        rows = slice(half * SPAN, half * SPAN + SPAN)
        delta = []
        for h in range(HEADS):
            cols = slice(h * HEAD_DIM, h * HEAD_DIM + HEAD_DIM)
            out = slice(h * SPAN, h * SPAN + SPAN)
            q_flat[half, out, :] = q_ref[rows, cols]
            g_flat[half, out, :] = g_ref[rows, cols]
            product = g_ref[rows, cols].astype(jnp.float32) * o_ref[rows, cols].astype(jnp.float32)
            delta.append(jnp.sum(product.T, axis=0, keepdims=True))
        stat[half, 0:1, :] = jnp.concatenate(
            [lse_ref[h : h + 1, rows] * LOG2E for h in range(HEADS)], axis=1
        )
        stat[half, 1:2, :] = jnp.concatenate(delta, axis=1)
        stat[half, 2:3, :] = jnp.concatenate(
            [start_ref[0:1, rows].astype(jnp.float32)] * HEADS, axis=1
        )
        stat[half, 3:4, :] = jnp.concatenate(
            [lax.broadcasted_iota(jnp.int32, (1, SPAN), 1).astype(jnp.float32)] * HEADS, axis=1
        )


def plan_kernel(table, spans, q0, q1, g0, g1, s0, s1, q_flat, g_flat, stat, plan):
    ctx, head = lax.axis_index("ctx"), lax.axis_index("head")
    base = (ctx * 2 + head % 2) * WIDTH
    for to, pair in ((q_flat, (q0, q1)), (g_flat, (g0, g1)), (stat, (s0, s1))):
        for side in range(2):
            to[2 * side : 2 * side + 2] = pair[side][...]
    first = []
    for qs in range(4):
        starts = (s0, s1)[qs // 2][qs % 2, 2:3, 0:SPAN]
        first.append(jnp.min(starts.astype(jnp.int32)))
    for n in range(8):
        plan[n * LIST] = 0
    for n in range(16):
        plan[KINDS + n] = table[base + 56 + n]
    begin = []
    for qs in range(4):
        begin.append(spans[table[base + qs]] * SPAN)
        plan[KINDS + 16 + qs] = begin[qs]

    @pl.loop(0, 16)
    def _(u):
        k_begin = spans[table[base + 8 + u]] * SPAN
        at_k, at_v = table[base + 24 + u], table[base + 40 + u]
        far = table[base + 72 + u]
        for qs in range(4):
            at = (far * 4 + qs) * LIST
            count = plan[at]
            plan[at + 1 + 3 * count] = at_k
            plan[at + 2 + 3 * count] = at_v
            plan[at + 3 + 3 * count] = k_begin
            meets = (k_begin <= begin[qs]) & (k_begin + (SPAN - 1) >= first[qs])
            plan[at] = count + meets.astype(jnp.int32)


def work(far, low, high, plan, q_flat, g_flat, stat, kv_all, dq_t, dkv):
    @pl.loop(low, high)
    def _(qs):
        at = (far * 4 + qs) * LIST
        count = plan[at]
        q_begin = plan[KINDS + 16 + qs]

        def stack(begin, size):
            at_k = [plan[at + 1 + 3 * (begin + j)] for j in range(size)]
            at_v = [plan[at + 2 + 3 * (begin + j)] for j in range(size)]
            k_begin = [plan[at + 3 + 3 * (begin + j)] for j in range(size)]
            key = jnp.concatenate([kv_all[n] for n in at_k], axis=0)
            value = jnp.concatenate([kv_all[n] for n in at_v], axis=0)
            q, g = q_flat[qs], g_flat[qs]
            lse, delta = stat[qs, 0:1, :], stat[qs, 1:2, :]
            start = stat[qs, 2:3, :].astype(jnp.int32)
            q_pos = stat[qs, 3:4, :].astype(jnp.int32) + q_begin
            s = lax.dot_general(key, q, NT, preferred_element_type=jnp.float32)
            dp = lax.dot_general(value, g, NT, preferred_element_type=jnp.float32)
            p = jnp.exp2(s * (SCALE * LOG2E) - lse)
            local = lax.broadcasted_iota(jnp.int32, (SPAN, FLAT), 0)
            masked = []
            for j in range(size):
                allowed = (local <= q_pos - k_begin[j]) & (local >= start - k_begin[j])
                masked.append(jnp.where(allowed, p[j * SPAN : (j + 1) * SPAN], 0.0))
            p = jnp.concatenate(masked, axis=0)
            ds = (p * (dp - delta)).astype(jnp.bfloat16)
            dv = jnp.dot(p.astype(jnp.bfloat16), g, preferred_element_type=jnp.float32)
            dk = jnp.dot(ds, q, preferred_element_type=jnp.float32)
            for j in range(size):
                dkv[at_v[j]] += dv[j * SPAN : (j + 1) * SPAN]
                dkv[at_k[j]] += dk[j * SPAN : (j + 1) * SPAN]
            dq_t[qs - low] += jnp.dot(key.T, ds, preferred_element_type=jnp.float32)

        @pl.loop(0, count // 4)
        def _(i):
            stack(4 * i, 4)

        @pl.when(count % 4 >= 2)
        def _():
            stack(count // 4 * 4, 2)

        @pl.when(count % 2 == 1)
        def _():
            stack(count - 1, 1)


def take(kv_all, at, refs):
    for ref in refs:
        for n in range(ref.shape[0]):
            kv_all[at] = ref[n, 0:SPAN]
            kv_all[at + 1] = ref[n, SPAN : 2 * SPAN]
            at += 2


def give(plan, dkv, at, refs):
    for ref in refs:
        for n in range(ref.shape[0]):
            factor = jnp.where(plan[KINDS + at] == 1, jnp.float32(SCALE), jnp.float32(1.0))
            for half in range(2):
                ref[n, half * SPAN : (half + 1) * SPAN] = (dkv[2 * at + half] * factor).astype(ref.dtype)
            at += 1


def own_kernel(plan, q_flat, g_flat, stat, own, up, down, dkv, dq_t, kv_all):
    dq_t[...] = jnp.zeros_like(dq_t)
    dkv[...] = jnp.zeros_like(dkv)
    take(kv_all, 0, (own, up, down))
    work(0, 0, 2, plan, q_flat, g_flat, stat, kv_all, dq_t, dkv)


def far_kernel(plan, q_flat, g_flat, stat, own, low, high, dq_in, dq_t, e0, d2_low, d2_high, kv_all, dkv):
    dq_t[0:2] = dq_in[...]
    dq_t[2:4] = jnp.zeros_like(dq_t[2:4])
    dkv[0:8] = jnp.zeros_like(dkv[0:8])
    dkv[24:32] = jnp.zeros_like(dkv[24:32])
    take(kv_all, 0, (own,))
    take(kv_all, 24, (low, high))
    work(1, 0, 4, plan, q_flat, g_flat, stat, kv_all, dq_t, dkv)
    give(plan, dkv, 12, (d2_low, d2_high))
    for n in range(8):
        e0[n] = dkv[n]


def other_kernel(
    plan, q_flat, g_flat, stat, own, up, down, dq_in, dkv_in, e0, dq_t, d0, d1, d3, kv_all, dkv
):
    dq_t[...] = dq_in[2:4]
    dkv[8:24] = dkv_in[8:24]
    for n in range(8):
        dkv[n] = dkv_in[n] + e0[n]
    take(kv_all, 0, (own, up, down))
    work(0, 2, 4, plan, q_flat, g_flat, stat, kv_all, dq_t, dkv)
    give(plan, dkv, 0, (d0, d1, d3))


def rows_kernel(dq_own, dq_got, dq):
    for half in range(2):
        flat = ((dq_own[half] + dq_got[half]) * SCALE).T.astype(dq.dtype)
        for h in range(HEADS):
            dq[pl.ds(half * SPAN, SPAN), pl.ds(h * HEAD_DIM, HEAD_DIM)] = flat[
                h * SPAN : (h + 1) * SPAN, :
            ]


def call(kernel, scalars, inputs, outs, scratch=(), scalar_out=None, flops=3_000_000_000):
    vmem = pl.BlockSpec(memory_space=pltpu.VMEM)
    smem = pl.BlockSpec(memory_space=pltpu.SMEM)
    out_specs = [vmem] * len(outs)
    if scalar_out is not None:
        outs, out_specs = [*outs, scalar_out], [*out_specs, smem]
    return pl.pallas_call(
        kernel,
        out_shape=tuple(jax.ShapeDtypeStruct(*out) for out in outs),
        in_specs=[smem] * len(scalars) + [vmem] * len(inputs),
        out_specs=tuple(out_specs),
        scratch_shapes=[pltpu.VMEM(*s) for s in scratch],
        compiler_params=pltpu.CompilerParams(vmem_limit_bytes=36 * 2**20),
        cost_estimate=pl.CostEstimate(
            flops=flops, bytes_accessed=flops // 300, transcendentals=0
        ),
    )(*scalars, *inputs)


def total(*arrays):
    return functools.reduce(lambda a, b: a + b, [a.astype(jnp.float32) for a in arrays])


def shards(queries, out_grad, outputs, lse, kv_pair, span_order, doc_start):
    rows, width = queries.shape
    table = jnp.asarray(layout_table())

    f32, b16 = jnp.float32, jnp.bfloat16
    pair, flat = ((2, FLAT, HEAD_DIM), b16), ((4, FLAT, HEAD_DIM), b16)
    half_sum, dq_sum = ((2, HEAD_DIM, FLAT), f32), ((4, HEAD_DIM, FLAT), f32)
    blocks = ((32, SPAN, HEAD_DIM), b16), ((32, SPAN, HEAD_DIM), f32)
    four, two = (4, rows, HEAD_DIM), (2, rows, HEAD_DIM)
    ring = [move(kv_pair[0], 1, 0), move(kv_pair[0], 2, 0), move(kv_pair[0], -1, 0)]
    q, g, stat, shard = call(
        prepare_kernel,
        (),
        (queries, out_grad, outputs, lse, jnp.broadcast_to(doc_start[None], (8, rows)), kv_pair[0]),
        [pair, pair, ((2, 4, FLAT), f32), ((rows, HEAD_DIM), b16)],
        flops=1_000_000_000,
    )
    ring, (q, g, stat, shard) = lax.optimization_barrier((ring, (q, g, stat, shard)))
    own = jnp.stack([shard, *ring])
    up, down = move(own, 0, 1), move(own, 0, -1)
    other = [other_core(v) for v in (stat, q, g)]
    *flats, plan = call(
        plan_kernel,
        (table, span_order),
        (q, other[1], g, other[2], stat, other[0]),
        [flat, flat, ((4, 4, FLAT), f32)],
        scalar_out=((KINDS + 20,), jnp.int32),
        flops=1_000_000_000,
    )
    up, down, flats, plan = lax.optimization_barrier((up, down, flats, plan))
    low, high = move(up[:2], 0, 1), move(down[2:], 0, -1)

    dkv, dq_own = call(
        own_kernel,
        (plan,),
        (*flats, own, up, down),
        [((24, SPAN, HEAD_DIM), f32), half_sum],
        blocks[:1],
    )
    dq_own, e0, d2_low, d2_high = call(
        far_kernel,
        (plan,),
        (*flats, own, low, high, dq_own),
        [dq_sum, ((8, SPAN, HEAD_DIM), f32), (two, b16), (two, b16)],
        blocks,
    )
    low, high = move(d2_low, 0, -1), move(d2_high, 0, 1)
    dq_send, d0, d1, d3 = call(
        other_kernel,
        (plan,),
        (*flats, own, up, down, dq_own, dkv, e0),
        [half_sum, (four, f32), (four, b16), (four, b16)],
        blocks,
    )

    low, high, d1, d3 = lax.optimization_barrier((low, high, d1, d3))
    d1 = jnp.concatenate([total(d1[:2], low).astype(b16), d1[2:]])
    d3 = jnp.concatenate([d3[:2], total(d3[2:], high).astype(b16)])
    d1, d3, dq_send = lax.optimization_barrier((d1, d3, dq_send))
    from_up, from_down = move(d1, 0, -1), move(d3, 0, 1)
    (dq,) = call(
        rows_kernel,
        (),
        (dq_own, other_core(dq_send)),
        [((rows, width), b16)],
        flops=1_000_000_000,
    )
    from_up, from_down, dq = lax.optimization_barrier((from_up, from_down, dq))
    ring = total(d0, from_up, from_down)
    sent = [ring[n].astype(b16) for n in (1, 2, 3)]
    kept = total(ring[0], move(sent[0], -1, 0), move(sent[2], 1, 0), move(sent[1], 2, 0))
    return dq, kept[None].astype(b16)


def solution(mesh):
    return jax.shard_map(
        shards,
        mesh=mesh,
        in_specs=(
            P("ctx", "head"),
            P("ctx", "head"),
            P("ctx", "head"),
            P("head", "ctx"),
            P("head", "ctx", None),
            P(),
            P("ctx"),
        ),
        out_specs=(P("ctx", "head"), P("head", "ctx", None)),
        check_vma=False,
    )
```

```python
import functools
import math

import jax
import jax.numpy as jnp
import numpy as np
from jax import lax
from jax.experimental import pallas as pl
from jax.experimental.pallas import tpu as pltpu
from jax.sharding import PartitionSpec as P

HEAD_DIM = 128
SPAN = 192
HEADS = 4
FLAT = HEADS * SPAN
WIDTH = 88
LIST = 49
KINDS = 16 * LIST
LOG2E = math.log2(math.e)
SCALE = 1.0 / math.sqrt(HEAD_DIM)
AXES = ("ctx", "head")
NT = (((1,), (1,)), ((), ()))


def device_index(x, y, core, z):
    ctx = (y % 2) * 8 + x * 2 + core
    head = z * 2 + y // 2
    return ctx * 16 + head


def places():
    return [(x, y, c, z) for z in range(8) for y in range(4) for x in range(4) for c in range(2)]


def shifted(x, y, core, step_a, step_b):
    dx, dy = (step_a, step_b) if core == 0 else (step_b, step_a)
    return (x + dx) % 4, (y + dy) % 4


def move(block, step_a, step_b):
    pairs = []
    for x, y, core, z in places():
        to_x, to_y = shifted(x, y, core, step_a, step_b)
        pairs.append((device_index(x, y, core, z), device_index(to_x, to_y, core, z)))
    return lax.ppermute(block, AXES, pairs)


def other_core(block):
    return lax.ppermute(block, "ctx", [(i, i ^ 1) for i in range(16)])


BLOCK_B = (0, 1, 3, 2)


def layout_table():
    table = np.zeros((32, WIDTH), np.int32)
    for x, y, core, z in places():
        ctx = (y % 2) * 8 + x * 2 + core
        row = table[ctx * 2 + y // 2]
        row[0:4] = [2 * ctx, 2 * ctx + 1, 2 * (ctx ^ 1), 2 * (ctx ^ 1) + 1]
        for n in range(16):
            step_b = BLOCK_B[n // 4]
            from_x, from_y = shifted(x, y, core, -(n % 4), -step_b)
            source = (from_y % 2) * 8 + from_x * 2 + core
            for half in range(2):
                unit = (source // 2) * 2 + half
                row[8 + unit] = 2 * source + half
                row[(24 if from_y < 2 else 40) + unit] = 2 * n + half
                row[72 + unit] |= step_b == 2
            row[56 + n] = from_y < 2
    return table.reshape(-1)


def prepare_kernel(g_ref, o_ref, lse_ref, start_ref, kv_ref, stat, kv):
    kv[...] = kv_ref[...]
    for half in range(2):
        rows = slice(half * SPAN, half * SPAN + SPAN)
        delta = []
        for h in range(HEADS):
            cols = slice(h * HEAD_DIM, h * HEAD_DIM + HEAD_DIM)
            product = g_ref[rows, cols].astype(jnp.float32) * o_ref[rows, cols].astype(jnp.float32)
            delta.append(jnp.sum(product.T, axis=0, keepdims=True))
        stat[half, 0:1, :] = jnp.concatenate(
            [lse_ref[h : h + 1, rows] * LOG2E for h in range(HEADS)], axis=1
        )
        stat[half, 1:2, :] = jnp.concatenate(delta, axis=1)
        stat[half, 2:3, :] = jnp.concatenate(
            [start_ref[0:1, rows].astype(jnp.float32)] * HEADS, axis=1
        )
        stat[half, 3:4, :] = jnp.concatenate(
            [lax.broadcasted_iota(jnp.int32, (1, SPAN), 1).astype(jnp.float32)] * HEADS, axis=1
        )


def plan_kernel(table, spans, q0, q1, g0, g1, s0, s1, q_flat, g_flat, stat, plan):
    ctx, head = lax.axis_index("ctx"), lax.axis_index("head")
    base = (ctx * 2 + head % 2) * WIDTH
    for side in range(2):
        stat[2 * side : 2 * side + 2] = (s0, s1)[side][...]
        for half in range(2):
            rows = slice(half * SPAN, half * SPAN + SPAN)
            for h in range(HEADS):
                cols = slice(h * HEAD_DIM, h * HEAD_DIM + HEAD_DIM)
                out = slice(h * SPAN, h * SPAN + SPAN)
                q_flat[2 * side + half, out, :] = (q0, q1)[side][rows, cols]
                g_flat[2 * side + half, out, :] = (g0, g1)[side][rows, cols]
    first, last = [], []
    for qs in range(4):
        starts = (s0, s1)[qs // 2][qs % 2, 2:3, 0:SPAN].astype(jnp.int32)
        first.append(jnp.min(starts))
        last.append(jnp.max(starts))
    for n in range(16):
        plan[n * LIST] = 0
    for n in range(16):
        plan[KINDS + n] = table[base + 56 + n]
    begin = []
    for qs in range(4):
        begin.append(spans[table[base + qs]] * SPAN)
        plan[KINDS + 16 + qs] = begin[qs]

    @pl.loop(0, 16)
    def _(u):
        k_begin = spans[table[base + 8 + u]] * SPAN
        at_k, at_v = table[base + 24 + u], table[base + 40 + u]
        far = table[base + 72 + u]
        for qs in range(4):
            whole = (k_begin < begin[qs]) & (k_begin >= last[qs])
            meets = (k_begin <= begin[qs]) & (k_begin + (SPAN - 1) >= first[qs])
            at = (far * 8 + qs * 2 + 1 - whole.astype(jnp.int32)) * LIST
            count = plan[at]
            plan[at + 1 + 3 * count] = at_k
            plan[at + 2 + 3 * count] = at_v
            plan[at + 3 + 3 * count] = k_begin
            plan[at] = count + meets.astype(jnp.int32)


def work(far, low, high, plan, q_flat, g_flat, stat, kv_all, dq_t, dkv):
    @pl.loop(low, high)
    def _(qs):
        at = (far * 8 + qs * 2) * LIST
        whole = plan[at]
        count = whole + plan[at + LIST]
        q_begin = plan[KINDS + 16 + qs]

        def stack(begin, size, mask):
            entries = [
                jnp.where(n < whole, at + 1 + 3 * n, at + LIST + 1 + 3 * (n - whole))
                for n in [begin + j for j in range(size)]
            ]
            at_k = [plan[n] for n in entries]
            at_v = [plan[n + 1] for n in entries]
            k_begin = [plan[n + 2] for n in entries]
            key = jnp.concatenate([kv_all[n] for n in at_k], axis=0)
            value = jnp.concatenate([kv_all[n] for n in at_v], axis=0)
            q, g = q_flat[qs], g_flat[qs]
            lse, delta = stat[qs, 0:1, :], stat[qs, 1:2, :]
            s = lax.dot_general(key, q, NT, preferred_element_type=jnp.float32)
            dp = lax.dot_general(value, g, NT, preferred_element_type=jnp.float32)
            p = jnp.exp2(s * (SCALE * LOG2E) - lse)
            if mask:
                start = stat[qs, 2:3, :].astype(jnp.int32)
                q_pos = stat[qs, 3:4, :].astype(jnp.int32) + q_begin
                local = lax.broadcasted_iota(jnp.int32, (SPAN, FLAT), 0)
                masked = []
                for j in range(size):
                    allowed = (local <= q_pos - k_begin[j]) & (local >= start - k_begin[j])
                    masked.append(jnp.where(allowed, p[j * SPAN : (j + 1) * SPAN], 0.0))
                p = jnp.concatenate(masked, axis=0)
            ds = (p * (dp - delta)).astype(jnp.bfloat16)
            dv = jnp.dot(p.astype(jnp.bfloat16), g, preferred_element_type=jnp.float32)
            dk = jnp.dot(ds, q, preferred_element_type=jnp.float32)
            for j in range(size):
                dkv[at_v[j]] += dv[j * SPAN : (j + 1) * SPAN]
                dkv[at_k[j]] += dk[j * SPAN : (j + 1) * SPAN]
            dq_t[qs - low] += jnp.dot(key.T, ds, preferred_element_type=jnp.float32)

        @pl.loop(0, whole // 4)
        def _(i):
            stack(4 * i, 4, False)

        @pl.loop(whole // 4, count // 4)
        def _(i):
            stack(4 * i, 4, True)

        for size in (3, 2, 1):

            @pl.when(count % 4 == size)
            def _():
                stack(count // 4 * 4, size, True)


def take(kv_all, at, refs):
    for ref in refs:
        for n in range(ref.shape[0]):
            kv_all[at] = ref[n, 0:SPAN]
            kv_all[at + 1] = ref[n, SPAN : 2 * SPAN]
            at += 2


def give(plan, dkv, at, refs):
    for ref in refs:
        for n in range(ref.shape[0]):
            factor = jnp.where(plan[KINDS + at] == 1, jnp.float32(SCALE), jnp.float32(1.0))
            for half in range(2):
                ref[n, half * SPAN : (half + 1) * SPAN] = (dkv[2 * at + half] * factor).astype(ref.dtype)
            at += 1


def own_kernel(plan, q_flat, g_flat, stat, own, up, down, dkv, dq_t, kv_all):
    dq_t[...] = jnp.zeros_like(dq_t)
    dkv[...] = jnp.zeros_like(dkv)
    take(kv_all, 0, (own, up, down))
    work(0, 0, 2, plan, q_flat, g_flat, stat, kv_all, dq_t, dkv)


def far_kernel(plan, q_flat, g_flat, stat, own, low, high, dq_in, dq_t, e0, d2_low, d2_high, kv_all, dkv):
    dq_t[0:2] = dq_in[...]
    dq_t[2:4] = jnp.zeros_like(dq_t[2:4])
    dkv[0:8] = jnp.zeros_like(dkv[0:8])
    dkv[24:32] = jnp.zeros_like(dkv[24:32])
    take(kv_all, 0, (own,))
    take(kv_all, 24, (low, high))
    work(1, 0, 4, plan, q_flat, g_flat, stat, kv_all, dq_t, dkv)
    give(plan, dkv, 12, (d2_low, d2_high))
    for n in range(8):
        e0[n] = dkv[n]


def other_kernel(
    plan, q_flat, g_flat, stat, own, up, down, dq_in, dkv_in, e0, dq_t, d0, d1, d3, kv_all, dkv
):
    dq_t[...] = dq_in[2:4]
    dkv[8:24] = dkv_in[8:24]
    for n in range(8):
        dkv[n] = dkv_in[n] + e0[n]
    take(kv_all, 0, (own, up, down))
    work(0, 2, 4, plan, q_flat, g_flat, stat, kv_all, dq_t, dkv)
    give(plan, dkv, 0, (d0, d1, d3))


def rows_kernel(dq_own, dq_got, dq):
    for half in range(2):
        flat = ((dq_own[half] + dq_got[half]) * SCALE).T.astype(dq.dtype)
        for h in range(HEADS):
            dq[pl.ds(half * SPAN, SPAN), pl.ds(h * HEAD_DIM, HEAD_DIM)] = flat[
                h * SPAN : (h + 1) * SPAN, :
            ]


def call(kernel, scalars, inputs, outs, scratch=(), scalar_out=None, flops=3_000_000_000):
    vmem = pl.BlockSpec(memory_space=pltpu.VMEM)
    smem = pl.BlockSpec(memory_space=pltpu.SMEM)
    out_specs = [vmem] * len(outs)
    if scalar_out is not None:
        outs, out_specs = [*outs, scalar_out], [*out_specs, smem]
    return pl.pallas_call(
        kernel,
        out_shape=tuple(jax.ShapeDtypeStruct(*out) for out in outs),
        in_specs=[smem] * len(scalars) + [vmem] * len(inputs),
        out_specs=tuple(out_specs),
        scratch_shapes=[pltpu.VMEM(*s) for s in scratch],
        compiler_params=pltpu.CompilerParams(vmem_limit_bytes=36 * 2**20),
        cost_estimate=pl.CostEstimate(
            flops=flops, bytes_accessed=flops // 300, transcendentals=0
        ),
    )(*scalars, *inputs)


def total(*arrays):
    return functools.reduce(lambda a, b: a + b, [a.astype(jnp.float32) for a in arrays])


def shards(queries, out_grad, outputs, lse, kv_pair, span_order, doc_start):
    rows, width = queries.shape
    table = jnp.asarray(layout_table())

    f32, b16 = jnp.float32, jnp.bfloat16
    flat = (4, FLAT, HEAD_DIM), b16
    half_sum, dq_sum = ((2, HEAD_DIM, FLAT), f32), ((4, HEAD_DIM, FLAT), f32)
    blocks = ((32, SPAN, HEAD_DIM), b16), ((32, SPAN, HEAD_DIM), f32)
    four, two = (4, rows, HEAD_DIM), (2, rows, HEAD_DIM)
    ring = [move(kv_pair[0], 1, 0), move(kv_pair[0], 2, 0), move(kv_pair[0], -1, 0)]
    stat, shard = call(
        prepare_kernel,
        (),
        (out_grad, outputs, lse, jnp.broadcast_to(doc_start[None], (8, rows)), kv_pair[0]),
        [((2, 4, FLAT), f32), ((rows, HEAD_DIM), b16)],
        flops=1_000_000_000,
    )
    ring, (stat, shard) = lax.optimization_barrier((ring, (stat, shard)))
    own = jnp.stack([shard, *ring])
    up, down = move(own, 0, 1), move(own, 0, -1)
    other = [other_core(v) for v in (stat, queries, out_grad)]
    *flats, plan = call(
        plan_kernel,
        (table, span_order),
        (queries, other[1], out_grad, other[2], stat, other[0]),
        [flat, flat, ((4, 4, FLAT), f32)],
        scalar_out=((KINDS + 20,), jnp.int32),
        flops=1_000_000_000,
    )
    up, down, flats, plan = lax.optimization_barrier((up, down, flats, plan))
    low, high = move(up[:2], 0, 1), move(down[2:], 0, -1)

    dkv, dq_own = call(
        own_kernel,
        (plan,),
        (*flats, own, up, down),
        [((24, SPAN, HEAD_DIM), f32), half_sum],
        blocks[:1],
    )
    dq_own, e0, d2_low, d2_high = call(
        far_kernel,
        (plan,),
        (*flats, own, low, high, dq_own),
        [dq_sum, ((8, SPAN, HEAD_DIM), f32), (two, b16), (two, b16)],
        blocks,
    )
    low, high = move(d2_low, 0, -1), move(d2_high, 0, 1)
    dq_send, d0, d1, d3 = call(
        other_kernel,
        (plan,),
        (*flats, own, up, down, dq_own, dkv, e0),
        [half_sum, (four, f32), (four, b16), (four, b16)],
        blocks,
    )

    low, high, d1, d3 = lax.optimization_barrier((low, high, d1, d3))
    d1 = jnp.concatenate([total(d1[:2], low).astype(b16), d1[2:]])
    d3 = jnp.concatenate([d3[:2], total(d3[2:], high).astype(b16)])
    d1, d3, dq_send = lax.optimization_barrier((d1, d3, dq_send))
    from_up, from_down = move(d1, 0, -1), move(d3, 0, 1)
    (dq,) = call(
        rows_kernel,
        (),
        (dq_own, other_core(dq_send)),
        [((rows, width), b16)],
        flops=1_000_000_000,
    )
    from_up, from_down, dq = lax.optimization_barrier((from_up, from_down, dq))
    ring = total(d0, from_up, from_down)
    sent = [ring[n].astype(b16) for n in (1, 2, 3)]
    kept = total(ring[0], move(sent[0], -1, 0), move(sent[2], 1, 0), move(sent[1], 2, 0))
    return dq, kept[None].astype(b16)


def solution(mesh):
    return jax.shard_map(
        shards,
        mesh=mesh,
        in_specs=(
            P("ctx", "head"),
            P("ctx", "head"),
            P("ctx", "head"),
            P("head", "ctx"),
            P("head", "ctx", None),
            P(),
            P("ctx"),
        ),
        out_specs=(P("ctx", "head"), P("head", "ctx", None)),
        check_vma=False,
    )
```

```python
import functools
import math

import jax
import jax.numpy as jnp
import numpy as np
from jax import lax
from jax.experimental import pallas as pl
from jax.experimental.pallas import tpu as pltpu
from jax.sharding import PartitionSpec as P

HEAD_DIM = 128
SPAN = 192
HEADS = 4
FLAT = HEADS * SPAN
WIDTH = 88
LIST = 49
KINDS = 16 * LIST
LOG2E = math.log2(math.e)
SCALE = 1.0 / math.sqrt(HEAD_DIM)
AXES = ("ctx", "head")
NT = (((1,), (1,)), ((), ()))


def device_index(x, y, core, z):
    ctx = (y % 2) * 8 + x * 2 + core
    head = z * 2 + y // 2
    return ctx * 16 + head


def places():
    return [(x, y, c, z) for z in range(8) for y in range(4) for x in range(4) for c in range(2)]


def shifted(x, y, core, step_a, step_b):
    dx, dy = (step_a, step_b) if core == 0 else (step_b, step_a)
    return (x + dx) % 4, (y + dy) % 4


def move(block, step_a, step_b):
    pairs = []
    for x, y, core, z in places():
        to_x, to_y = shifted(x, y, core, step_a, step_b)
        pairs.append((device_index(x, y, core, z), device_index(to_x, to_y, core, z)))
    return lax.ppermute(block, AXES, pairs)


def other_core(block):
    return lax.ppermute(block, "ctx", [(i, i ^ 1) for i in range(16)])


BLOCK_B = (0, 1, 3, 2)


def layout_table():
    table = np.zeros((32, WIDTH), np.int32)
    for x, y, core, z in places():
        ctx = (y % 2) * 8 + x * 2 + core
        row = table[ctx * 2 + y // 2]
        row[0:4] = [2 * ctx, 2 * ctx + 1, 2 * (ctx ^ 1), 2 * (ctx ^ 1) + 1]
        for n in range(16):
            step_b = BLOCK_B[n // 4]
            from_x, from_y = shifted(x, y, core, -(n % 4), -step_b)
            source = (from_y % 2) * 8 + from_x * 2 + core
            for half in range(2):
                unit = (source // 2) * 2 + half
                row[8 + unit] = 2 * source + half
                row[(24 if from_y < 2 else 40) + unit] = 2 * n + half
                row[72 + unit] |= step_b == 2
            row[56 + n] = from_y < 2
    return table.reshape(-1)


def prepare_kernel(g_ref, o_ref, lse_ref, start_ref, kv_ref, stat, kv):
    kv[...] = kv_ref[...]
    for half in range(2):
        rows = slice(half * SPAN, half * SPAN + SPAN)
        delta = []
        for h in range(HEADS):
            cols = slice(h * HEAD_DIM, h * HEAD_DIM + HEAD_DIM)
            product = g_ref[rows, cols].astype(jnp.float32) * o_ref[rows, cols].astype(jnp.float32)
            delta.append(jnp.sum(product.T, axis=0, keepdims=True))
        stat[half, 0:1, :] = jnp.concatenate(
            [lse_ref[h : h + 1, rows] * LOG2E for h in range(HEADS)], axis=1
        )
        stat[half, 1:2, :] = jnp.concatenate(delta, axis=1)
        stat[half, 2:3, :] = jnp.concatenate(
            [start_ref[0:1, rows].astype(jnp.float32)] * HEADS, axis=1
        )
        stat[half, 3:4, :] = jnp.concatenate(
            [lax.broadcasted_iota(jnp.int32, (1, SPAN), 1).astype(jnp.float32)] * HEADS, axis=1
        )


def plan_kernel(table, spans, q0, q1, g0, g1, s0, s1, q_flat, g_flat, stat, plan):
    ctx, head = lax.axis_index("ctx"), lax.axis_index("head")
    base = (ctx * 2 + head % 2) * WIDTH
    for side in range(2):
        stat[2 * side : 2 * side + 2] = (s0, s1)[side][...]
        for half in range(2):
            rows = slice(half * SPAN, half * SPAN + SPAN)
            for h in range(HEADS):
                cols = slice(h * HEAD_DIM, h * HEAD_DIM + HEAD_DIM)
                out = slice(h * SPAN, h * SPAN + SPAN)
                q_flat[2 * side + half, out, :] = (q0, q1)[side][rows, cols]
                g_flat[2 * side + half, out, :] = (g0, g1)[side][rows, cols]
    first, last = [], []
    for qs in range(4):
        starts = (s0, s1)[qs // 2][qs % 2, 2:3, 0:SPAN].astype(jnp.int32)
        first.append(jnp.min(starts))
        last.append(jnp.max(starts))
    for n in range(16):
        plan[n * LIST] = 0
    for n in range(16):
        plan[KINDS + n] = table[base + 56 + n]
    begin = []
    for qs in range(4):
        begin.append(spans[table[base + qs]] * SPAN)
        plan[KINDS + 16 + qs] = begin[qs]

    @pl.loop(0, 16)
    def _(u):
        k_begin = spans[table[base + 8 + u]] * SPAN
        at_k, at_v = table[base + 24 + u], table[base + 40 + u]
        far = table[base + 72 + u]
        for qs in range(4):
            whole = (k_begin < begin[qs]) & (k_begin >= last[qs])
            meets = (k_begin <= begin[qs]) & (k_begin + (SPAN - 1) >= first[qs])
            at = (far * 8 + qs * 2 + 1 - whole.astype(jnp.int32)) * LIST
            count = plan[at]
            plan[at + 1 + 3 * count] = at_k
            plan[at + 2 + 3 * count] = at_v
            plan[at + 3 + 3 * count] = k_begin
            plan[at] = count + meets.astype(jnp.int32)


def work(far, low, high, plan, q_flat, g_flat, stat, kv_all, dq_t, dkv):
    @pl.loop(low, high)
    def _(qs):
        at = (far * 8 + qs * 2) * LIST
        whole = plan[at]
        count = whole + plan[at + LIST]
        q_begin = plan[KINDS + 16 + qs]

        def stack(begin, size, mask):
            entries = [
                jnp.where(n < whole, at + 1 + 3 * n, at + LIST + 1 + 3 * (n - whole))
                for n in [begin + j for j in range(size)]
            ]
            at_k = [plan[n] for n in entries]
            at_v = [plan[n + 1] for n in entries]
            k_begin = [plan[n + 2] for n in entries]
            key = jnp.concatenate([kv_all[n] for n in at_k], axis=0)
            value = jnp.concatenate([kv_all[n] for n in at_v], axis=0)
            q, g = q_flat[qs], g_flat[qs]
            lse, delta = stat[qs, 0:1, :], stat[qs, 1:2, :]
            s = lax.dot_general(key, q, NT, preferred_element_type=jnp.float32)
            dp = lax.dot_general(value, g, NT, preferred_element_type=jnp.float32)
            p = jnp.exp2(s * (SCALE * LOG2E) - lse)
            if mask:
                start = stat[qs, 2:3, :].astype(jnp.int32)
                q_pos = stat[qs, 3:4, :].astype(jnp.int32) + q_begin
                local = lax.broadcasted_iota(jnp.int32, (SPAN, FLAT), 0)
                masked = []
                for j in range(size):
                    allowed = (local <= q_pos - k_begin[j]) & (local >= start - k_begin[j])
                    masked.append(jnp.where(allowed, p[j * SPAN : (j + 1) * SPAN], 0.0))
                p = jnp.concatenate(masked, axis=0)
            ds = (p * (dp - delta)).astype(jnp.bfloat16)
            dv = jnp.dot(p.astype(jnp.bfloat16), g, preferred_element_type=jnp.float32)
            dk = jnp.dot(ds, q, preferred_element_type=jnp.float32)
            for j in range(size):
                dkv[at_v[j]] += dv[j * SPAN : (j + 1) * SPAN]
                dkv[at_k[j]] += dk[j * SPAN : (j + 1) * SPAN]
            dq_t[qs - low] += jnp.dot(key.T, ds, preferred_element_type=jnp.float32)

        @pl.loop(0, whole // 4)
        def _(i):
            stack(4 * i, 4, False)

        @pl.loop(whole // 4, count // 4)
        def _(i):
            stack(4 * i, 4, True)

        for size in (3, 2, 1):

            @pl.when(count % 4 == size)
            def _():
                stack(count // 4 * 4, size, True)


def take(kv_all, at, refs):
    for ref in refs:
        for n in range(ref.shape[0]):
            kv_all[at] = ref[n, 0:SPAN]
            kv_all[at + 1] = ref[n, SPAN : 2 * SPAN]
            at += 2


def give(plan, dkv, at, refs):
    for ref in refs:
        for n in range(ref.shape[0]):
            factor = jnp.where(plan[KINDS + at] == 1, jnp.float32(SCALE), jnp.float32(1.0))
            for half in range(2):
                ref[n, half * SPAN : (half + 1) * SPAN] = (dkv[2 * at + half] * factor).astype(ref.dtype)
            at += 1


def own_kernel(plan, q_flat, g_flat, stat, own, up, down, dkv, dq_t, kv_all):
    dq_t[...] = jnp.zeros_like(dq_t)
    dkv[...] = jnp.zeros_like(dkv)
    take(kv_all, 0, (own, up, down))
    work(0, 0, 2, plan, q_flat, g_flat, stat, kv_all, dq_t, dkv)


def far_kernel(plan, q_flat, g_flat, stat, own, low, high, dq_in, dq_t, e0, d2_low, d2_high, kv_all, dkv):
    dq_t[0:2] = dq_in[...]
    dq_t[2:4] = jnp.zeros_like(dq_t[2:4])
    dkv[0:8] = jnp.zeros_like(dkv[0:8])
    dkv[24:32] = jnp.zeros_like(dkv[24:32])
    take(kv_all, 0, (own,))
    take(kv_all, 24, (low, high))
    work(1, 0, 4, plan, q_flat, g_flat, stat, kv_all, dq_t, dkv)
    give(plan, dkv, 12, (d2_low, d2_high))
    for n in range(8):
        e0[n] = dkv[n]


def other_kernel(
    plan, q_flat, g_flat, stat, own, up, down, dq_in, dkv_in, e0, dq_t, d0, d1, d3, kv_all, dkv
):
    dq_t[...] = dq_in[2:4]
    dkv[8:24] = dkv_in[8:24]
    for n in range(8):
        dkv[n] = dkv_in[n] + e0[n]
    take(kv_all, 0, (own, up, down))
    work(0, 2, 4, plan, q_flat, g_flat, stat, kv_all, dq_t, dkv)
    give(plan, dkv, 0, (d0, d1, d3))


def rows_kernel(dq_own, dq_got, dq):
    for half in range(2):
        flat = ((dq_own[half] + dq_got[half]) * SCALE).T.astype(dq.dtype)
        for h in range(HEADS):
            dq[pl.ds(half * SPAN, SPAN), pl.ds(h * HEAD_DIM, HEAD_DIM)] = flat[
                h * SPAN : (h + 1) * SPAN, :
            ]


def call(kernel, scalars, inputs, outs, scratch=(), scalar_out=None, flops=3_000_000_000):
    vmem = pl.BlockSpec(memory_space=pltpu.VMEM)
    smem = pl.BlockSpec(memory_space=pltpu.SMEM)
    out_specs = [vmem] * len(outs)
    if scalar_out is not None:
        outs, out_specs = [*outs, scalar_out], [*out_specs, smem]
    return pl.pallas_call(
        kernel,
        out_shape=tuple(jax.ShapeDtypeStruct(*out) for out in outs),
        in_specs=[smem] * len(scalars) + [vmem] * len(inputs),
        out_specs=tuple(out_specs),
        scratch_shapes=[pltpu.VMEM(*s) for s in scratch],
        compiler_params=pltpu.CompilerParams(vmem_limit_bytes=36 * 2**20),
        cost_estimate=pl.CostEstimate(
            flops=flops, bytes_accessed=flops // 300, transcendentals=0
        ),
    )(*scalars, *inputs)


def total(*arrays):
    return functools.reduce(lambda a, b: a + b, [a.astype(jnp.float32) for a in arrays])


def shards(queries, out_grad, outputs, lse, kv_pair, span_order, doc_start):
    rows, width = queries.shape
    table = jnp.asarray(layout_table())

    f32, b16 = jnp.float32, jnp.bfloat16
    flat = (4, FLAT, HEAD_DIM), b16
    half_sum, dq_sum = ((2, HEAD_DIM, FLAT), f32), ((4, HEAD_DIM, FLAT), f32)
    blocks = ((32, SPAN, HEAD_DIM), b16), ((32, SPAN, HEAD_DIM), f32)
    four, two = (4, rows, HEAD_DIM), (2, rows, HEAD_DIM)
    ring = [move(kv_pair[0], 1, 0), move(kv_pair[0], 2, 0), move(kv_pair[0], -1, 0)]
    stat, shard = call(
        prepare_kernel,
        (),
        (out_grad, outputs, lse, jnp.broadcast_to(doc_start[None], (8, rows)), kv_pair[0]),
        [((2, 4, FLAT), f32), ((rows, HEAD_DIM), b16)],
        flops=1_000_000_000,
    )
    ring, (stat, shard) = lax.optimization_barrier((ring, (stat, shard)))
    own = jnp.stack([shard, *ring])
    up, down = move(own, 0, 1), move(own, 0, -1)
    other = [other_core(v) for v in (stat, queries, out_grad)]
    *flats, plan = call(
        plan_kernel,
        (table, span_order),
        (queries, other[1], out_grad, other[2], stat, other[0]),
        [flat, flat, ((4, 4, FLAT), f32)],
        scalar_out=((KINDS + 20,), jnp.int32),
        flops=1_000_000_000,
    )
    up, down, flats, plan = lax.optimization_barrier((up, down, flats, plan))
    low, high = move(up[:2], 0, 1), move(down[2:], 0, -1)

    dkv, dq_own = call(
        own_kernel,
        (plan,),
        (*flats, own, up, down),
        [((24, SPAN, HEAD_DIM), f32), half_sum],
        blocks[:1],
    )
    dq_own, e0, d2_low, d2_high = call(
        far_kernel,
        (plan,),
        (*flats, own, low, high, dq_own),
        [dq_sum, ((8, SPAN, HEAD_DIM), f32), (two, b16), (two, b16)],
        blocks,
    )
    low, high = move(d2_low, 0, -1), move(d2_high, 0, 1)
    dq_send, d0, d1, d3 = call(
        other_kernel,
        (plan,),
        (*flats, own, up, down, dq_own, dkv, e0),
        [half_sum, (four, f32), (four, b16), (four, b16)],
        blocks,
    )

    low, high, d1, d3 = lax.optimization_barrier((low, high, d1, d3))
    d1 = jnp.concatenate([total(d1[:2], low).astype(b16), d1[2:]])
    d3 = jnp.concatenate([d3[:2], total(d3[2:], high).astype(b16)])
    from_up, from_down = move(d1, 0, -1), move(d3, 0, 1)
    from_up, from_down, dq_send = lax.optimization_barrier((from_up, from_down, dq_send))
    (dq,) = call(
        rows_kernel,
        (),
        (dq_own, other_core(dq_send)),
        [((rows, width), b16)],
        flops=1_000_000_000,
    )
    ring = total(d0, from_up, from_down)
    sent = [ring[n].astype(b16) for n in (1, 2, 3)]
    moved = move(sent[0], -1, 0), move(sent[2], 1, 0), move(sent[1], 2, 0)
    moved, dq = lax.optimization_barrier((moved, dq))
    kept = total(ring[0], *moved)
    return dq, kept[None].astype(b16)


def solution(mesh):
    return jax.shard_map(
        shards,
        mesh=mesh,
        in_specs=(
            P("ctx", "head"),
            P("ctx", "head"),
            P("ctx", "head"),
            P("head", "ctx"),
            P("head", "ctx", None),
            P(),
            P("ctx"),
        ),
        out_specs=(P("ctx", "head"), P("head", "ctx", None)),
        check_vma=False,
    )
```

```python
import functools
import math

import jax
import jax.numpy as jnp
import numpy as np
from jax import lax
from jax.experimental import pallas as pl
from jax.experimental.pallas import tpu as pltpu
from jax.sharding import PartitionSpec as P

HEAD_DIM = 128
SPAN = 192
HEADS = 4
FLAT = HEADS * SPAN
WIDTH = 88
LIST = 49
KINDS = 16 * LIST
LOG2E = math.log2(math.e)
SCALE = 1.0 / math.sqrt(HEAD_DIM)
AXES = ("ctx", "head")
NT = (((1,), (1,)), ((), ()))


def device_index(x, y, core, z):
    ctx = (y % 2) * 8 + x * 2 + core
    head = z * 2 + y // 2
    return ctx * 16 + head


def places():
    return [(x, y, c, z) for z in range(8) for y in range(4) for x in range(4) for c in range(2)]


def shifted(x, y, core, step_a, step_b):
    dx, dy = (step_a, step_b) if core == 0 else (step_b, step_a)
    return (x + dx) % 4, (y + dy) % 4


def move(block, step_a, step_b):
    pairs = []
    for x, y, core, z in places():
        to_x, to_y = shifted(x, y, core, step_a, step_b)
        pairs.append((device_index(x, y, core, z), device_index(to_x, to_y, core, z)))
    return lax.ppermute(block, AXES, pairs)


def other_core(block):
    return lax.ppermute(block, "ctx", [(i, i ^ 1) for i in range(16)])


BLOCK_B = (0, 1, 3, 2)


def layout_table():
    table = np.zeros((32, WIDTH), np.int32)
    for x, y, core, z in places():
        ctx = (y % 2) * 8 + x * 2 + core
        row = table[ctx * 2 + y // 2]
        row[0:4] = [2 * ctx, 2 * ctx + 1, 2 * (ctx ^ 1), 2 * (ctx ^ 1) + 1]
        for n in range(16):
            step_b = BLOCK_B[n // 4]
            from_x, from_y = shifted(x, y, core, -(n % 4), -step_b)
            source = (from_y % 2) * 8 + from_x * 2 + core
            for half in range(2):
                unit = (source // 2) * 2 + half
                row[8 + unit] = 2 * source + half
                row[(24 if from_y < 2 else 40) + unit] = 2 * n + half
                row[72 + unit] |= step_b == 2
            row[56 + n] = from_y < 2
    return table.reshape(-1)


def prepare_kernel(g_ref, o_ref, lse_ref, start_ref, kv_ref, stat, kv):
    kv[...] = kv_ref[...]
    for half in range(2):
        rows = slice(half * SPAN, half * SPAN + SPAN)
        delta = []
        for h in range(HEADS):
            cols = slice(h * HEAD_DIM, h * HEAD_DIM + HEAD_DIM)
            product = g_ref[rows, cols].astype(jnp.float32) * o_ref[rows, cols].astype(jnp.float32)
            delta.append(jnp.sum(product.T, axis=0, keepdims=True))
        stat[half, 0:1, :] = jnp.concatenate(
            [lse_ref[h : h + 1, rows] * LOG2E for h in range(HEADS)], axis=1
        )
        stat[half, 1:2, :] = jnp.concatenate(delta, axis=1)
        stat[half, 2:3, :] = jnp.concatenate(
            [start_ref[0:1, rows].astype(jnp.float32)] * HEADS, axis=1
        )
        stat[half, 3:4, :] = jnp.concatenate(
            [lax.broadcasted_iota(jnp.int32, (1, SPAN), 1).astype(jnp.float32)] * HEADS, axis=1
        )


def plan_kernel(table, spans, q0, q1, g0, g1, s0, s1, q_flat, g_flat, stat, plan):
    ctx, head = lax.axis_index("ctx"), lax.axis_index("head")
    base = (ctx * 2 + head % 2) * WIDTH
    for side in range(2):
        stat[2 * side : 2 * side + 2] = (s0, s1)[side][...]
        for half in range(2):
            rows = slice(half * SPAN, half * SPAN + SPAN)
            for h in range(HEADS):
                cols = slice(h * HEAD_DIM, h * HEAD_DIM + HEAD_DIM)
                out = slice(h * SPAN, h * SPAN + SPAN)
                q_flat[2 * side + half, out, :] = (q0, q1)[side][rows, cols]
                g_flat[2 * side + half, out, :] = (g0, g1)[side][rows, cols]
    first, last = [], []
    for qs in range(4):
        starts = (s0, s1)[qs // 2][qs % 2, 2:3, 0:SPAN].astype(jnp.int32)
        first.append(jnp.min(starts))
        last.append(jnp.max(starts))
    for n in range(16):
        plan[n * LIST] = 0
    for n in range(16):
        plan[KINDS + n] = table[base + 56 + n]
    begin = []
    for qs in range(4):
        begin.append(spans[table[base + qs]] * SPAN)
        plan[KINDS + 16 + qs] = begin[qs]

    @pl.loop(0, 16)
    def _(u):
        k_begin = spans[table[base + 8 + u]] * SPAN
        at_k, at_v = table[base + 24 + u], table[base + 40 + u]
        far = table[base + 72 + u]
        for qs in range(4):
            whole = (k_begin < begin[qs]) & (k_begin >= last[qs])
            meets = (k_begin <= begin[qs]) & (k_begin + (SPAN - 1) >= first[qs])
            at = (far * 8 + qs * 2 + 1 - whole.astype(jnp.int32)) * LIST
            count = plan[at]
            plan[at + 1 + 3 * count] = at_k
            plan[at + 2 + 3 * count] = at_v
            plan[at + 3 + 3 * count] = k_begin
            plan[at] = count + meets.astype(jnp.int32)


def work(far, low, high, plan, q_flat, g_flat, stat, kv_all, dq_t, dkv):
    @pl.loop(low, high)
    def _(qs):
        at = (far * 8 + qs * 2) * LIST
        whole = plan[at]
        count = whole + plan[at + LIST]
        q_begin = plan[KINDS + 16 + qs]

        def stack(begin, size, mask):
            entries = [
                jnp.where(n < whole, at + 1 + 3 * n, at + LIST + 1 + 3 * (n - whole))
                for n in [begin + j for j in range(size)]
            ]
            at_k = [plan[n] for n in entries]
            at_v = [plan[n + 1] for n in entries]
            k_begin = [plan[n + 2] for n in entries]
            key = jnp.concatenate([kv_all[n] for n in at_k], axis=0)
            value = jnp.concatenate([kv_all[n] for n in at_v], axis=0)
            q, g = q_flat[qs], g_flat[qs]
            lse, delta = stat[qs, 0:1, :], stat[qs, 1:2, :]
            s = lax.dot_general(key, q, NT, preferred_element_type=jnp.float32)
            dp = lax.dot_general(value, g, NT, preferred_element_type=jnp.float32)
            p = jnp.exp2(s * (SCALE * LOG2E) - lse)
            if mask:
                start = stat[qs, 2:3, :].astype(jnp.int32)
                q_pos = stat[qs, 3:4, :].astype(jnp.int32) + q_begin
                local = lax.broadcasted_iota(jnp.int32, (SPAN, FLAT), 0)
                masked = []
                for j in range(size):
                    allowed = (local <= q_pos - k_begin[j]) & (local >= start - k_begin[j])
                    masked.append(jnp.where(allowed, p[j * SPAN : (j + 1) * SPAN], 0.0))
                p = jnp.concatenate(masked, axis=0)
            ds = (p * (dp - delta)).astype(jnp.bfloat16)
            dv = jnp.dot(p.astype(jnp.bfloat16), g, preferred_element_type=jnp.float32)
            dk = jnp.dot(ds, q, preferred_element_type=jnp.float32)
            for j in range(size):
                dkv[at_v[j]] += dv[j * SPAN : (j + 1) * SPAN]
                dkv[at_k[j]] += dk[j * SPAN : (j + 1) * SPAN]
            dq_t[qs - low] += jnp.dot(key.T, ds, preferred_element_type=jnp.float32)

        @pl.loop(0, whole // 4)
        def _(i):
            stack(4 * i, 4, False)

        @pl.loop(whole // 4, count // 4)
        def _(i):
            stack(4 * i, 4, True)

        for size in (3, 2, 1):

            @pl.when(count % 4 == size)
            def _():
                stack(count // 4 * 4, size, True)


def take(kv_all, at, refs):
    for ref in refs:
        for n in range(ref.shape[0]):
            kv_all[at] = ref[n, 0:SPAN]
            kv_all[at + 1] = ref[n, SPAN : 2 * SPAN]
            at += 2


def give(plan, dkv, at, refs):
    for ref in refs:
        for n in range(ref.shape[0]):
            factor = jnp.where(plan[KINDS + at] == 1, jnp.float32(SCALE), jnp.float32(1.0))
            for half in range(2):
                ref[n, half * SPAN : (half + 1) * SPAN] = (dkv[2 * at + half] * factor).astype(ref.dtype)
            at += 1


def own_kernel(plan, q_flat, g_flat, stat, own, up, down, dkv, dq_t, kv_all):
    dq_t[...] = jnp.zeros_like(dq_t)
    dkv[...] = jnp.zeros_like(dkv)
    take(kv_all, 0, (own, up, down))
    work(0, 0, 2, plan, q_flat, g_flat, stat, kv_all, dq_t, dkv)


def far_kernel(plan, q_flat, g_flat, stat, own, low, high, dq_in, dq_t, e0, d2_low, d2_high, kv_all, dkv):
    dq_t[0:2] = dq_in[...]
    dq_t[2:4] = jnp.zeros_like(dq_t[2:4])
    dkv[0:8] = jnp.zeros_like(dkv[0:8])
    dkv[24:32] = jnp.zeros_like(dkv[24:32])
    take(kv_all, 0, (own,))
    take(kv_all, 24, (low, high))
    work(1, 0, 4, plan, q_flat, g_flat, stat, kv_all, dq_t, dkv)
    give(plan, dkv, 12, (d2_low, d2_high))
    for n in range(8):
        e0[n] = dkv[n]


def other_kernel(
    plan, q_flat, g_flat, stat, own, up, down, dq_in, dkv_in, e0, dq_t, d0, d1, d3, kv_all, dkv
):
    dq_t[...] = dq_in[2:4]
    dkv[8:24] = dkv_in[8:24]
    for n in range(8):
        dkv[n] = dkv_in[n] + e0[n]
    take(kv_all, 0, (own, up, down))
    work(0, 2, 4, plan, q_flat, g_flat, stat, kv_all, dq_t, dkv)
    give(plan, dkv, 0, (d0, d1, d3))


def rows_kernel(dq_own, dq_got, dq):
    for half in range(2):
        flat = ((dq_own[half] + dq_got[half]) * SCALE).T.astype(dq.dtype)
        for h in range(HEADS):
            dq[pl.ds(half * SPAN, SPAN), pl.ds(h * HEAD_DIM, HEAD_DIM)] = flat[
                h * SPAN : (h + 1) * SPAN, :
            ]


def call(kernel, scalars, inputs, outs, scratch=(), scalar_out=None, flops=3_000_000_000):
    vmem = pl.BlockSpec(memory_space=pltpu.VMEM)
    smem = pl.BlockSpec(memory_space=pltpu.SMEM)
    out_specs = [vmem] * len(outs)
    if scalar_out is not None:
        outs, out_specs = [*outs, scalar_out], [*out_specs, smem]
    return pl.pallas_call(
        kernel,
        out_shape=tuple(jax.ShapeDtypeStruct(*out) for out in outs),
        in_specs=[smem] * len(scalars) + [vmem] * len(inputs),
        out_specs=tuple(out_specs),
        scratch_shapes=[pltpu.VMEM(*s) for s in scratch],
        compiler_params=pltpu.CompilerParams(vmem_limit_bytes=36 * 2**20),
        cost_estimate=pl.CostEstimate(
            flops=flops, bytes_accessed=flops // 300, transcendentals=0
        ),
    )(*scalars, *inputs)


def total(*arrays):
    return functools.reduce(lambda a, b: a + b, [a.astype(jnp.float32) for a in arrays])


def shards(queries, out_grad, outputs, lse, kv_pair, span_order, doc_start):
    rows, width = queries.shape
    table = jnp.asarray(layout_table())

    f32, b16 = jnp.float32, jnp.bfloat16
    flat = (4, FLAT, HEAD_DIM), b16
    half_sum, dq_sum = ((2, HEAD_DIM, FLAT), f32), ((4, HEAD_DIM, FLAT), f32)
    blocks = ((32, SPAN, HEAD_DIM), b16), ((32, SPAN, HEAD_DIM), f32)
    four, two = (4, rows, HEAD_DIM), (2, rows, HEAD_DIM)
    ring_up, ring_down = move(kv_pair[0], 1, 0), move(kv_pair[0], -1, 0)
    ring = [ring_up, move(kv_pair[0], 2, 0), ring_down]
    stat, shard = call(
        prepare_kernel,
        (),
        (out_grad, outputs, lse, jnp.broadcast_to(doc_start[None], (8, rows)), kv_pair[0]),
        [((2, 4, FLAT), f32), ((rows, HEAD_DIM), b16)],
        flops=1_000_000_000,
    )
    ring, (stat, shard) = lax.optimization_barrier((ring, (stat, shard)))
    own = jnp.stack([shard, *ring])
    up, down = move(own, 0, 1), move(own, 0, -1)
    other = [other_core(v) for v in (stat, queries, out_grad)]
    *flats, plan = call(
        plan_kernel,
        (table, span_order),
        (queries, other[1], out_grad, other[2], stat, other[0]),
        [flat, flat, ((4, 4, FLAT), f32)],
        scalar_out=((KINDS + 20,), jnp.int32),
        flops=1_000_000_000,
    )
    up, down, flats, plan = lax.optimization_barrier((up, down, flats, plan))
    low, high = move(up[:2], 0, 1), move(down[2:], 0, -1)

    dkv, dq_own = call(
        own_kernel,
        (plan,),
        (*flats, own, up, down),
        [((24, SPAN, HEAD_DIM), f32), half_sum],
        blocks[:1],
    )
    dq_own, e0, d2_low, d2_high = call(
        far_kernel,
        (plan,),
        (*flats, own, low, high, dq_own),
        [dq_sum, ((8, SPAN, HEAD_DIM), f32), (two, b16), (two, b16)],
        blocks,
    )
    low, high = move(d2_low, 0, -1), move(d2_high, 0, 1)
    dq_send, d0, d1, d3 = call(
        other_kernel,
        (plan,),
        (*flats, own, up, down, dq_own, dkv, e0),
        [half_sum, (four, f32), (four, b16), (four, b16)],
        blocks,
    )

    low, high, d1, d3 = lax.optimization_barrier((low, high, d1, d3))
    d1 = jnp.concatenate([total(d1[:2], low).astype(b16), d1[2:]])
    d3 = jnp.concatenate([d3[:2], total(d3[2:], high).astype(b16)])
    from_up, from_down = move(d1, 0, -1), move(d3, 0, 1)
    from_up, from_down, dq_send = lax.optimization_barrier((from_up, from_down, dq_send))
    (dq,) = call(
        rows_kernel,
        (),
        (dq_own, other_core(dq_send)),
        [((rows, width), b16)],
        flops=1_000_000_000,
    )
    ring = total(d0, from_up, from_down)
    sent = [ring[n].astype(b16) for n in (1, 2, 3)]
    moved = move(sent[0], -1, 0), move(sent[2], 1, 0), move(sent[1], 2, 0)
    moved, dq = lax.optimization_barrier((moved, dq))
    kept = total(ring[0], *moved)
    return dq, kept[None].astype(b16)


def solution(mesh):
    return jax.shard_map(
        shards,
        mesh=mesh,
        in_specs=(
            P("ctx", "head"),
            P("ctx", "head"),
            P("ctx", "head"),
            P("head", "ctx"),
            P("head", "ctx", None),
            P(),
            P("ctx"),
        ),
        out_specs=(P("ctx", "head"), P("head", "ctx", None)),
        check_vma=False,
    )
```
